512 devices in a mesh: pool: 64 (over x, z), tensor: 8 (over y, core).
Axes of the slice: x: 4, y: 4, z: 16, core: 2. Of those that a mesh axis runs over, the one named last changes fastest.
Arguments:
- kv_pool: bfloat16 [1024, 8, 256, 256], P('pool', 'tensor'), may hold values from -6 to 6
- queries: bfloat16 [2, 64, 64, 128], P(None, 'pool', 'tensor'), may hold values from -1200 to 1200
- new_kv: bfloat16 [2, 64, 8, 256], P(None, 'pool', 'tensor'), may hold values from -6 to 6
- block_count: int32 [64], replicated, may hold values from 1 to 64, 1024 in all
- tail_gap: int32 [64], replicated, may hold values from 0 to 253
- block_place: int32 [1024], replicated, may hold values from 0 to 1023, each once
- out_weight: bfloat16 [8192, 8192], P('tensor', 'pool'), may hold values from -1 to 1
Outputs:
- projected: bfloat16 [2, 64, 8192], P(None, 'tensor', 'pool')
The draws below stay inside these ranges and needn't reach their ends.
Inputs may be any that keep to these rules, and one draw needn't show every extreme that they name: `block_count`: every request has 1 to 64 blocks, together exactly 1024, and one request has exactly 64. `block_place`: each global block appears exactly once.
All inputs are finite; a program needn't handle non-finite values.
Results may differ from the reference program's by a relative error of at most 0.0055.
Values may be sent and summed in bfloat16 or wider, within the bound.
A program may use at most 64 MiB of HBM per device.

```python
import math
import jax
import jax.numpy as jnp
import numpy as np

D = 8192
H = 64
KVH = 8
HD = 128
BT = 256
MAXB = 64
NBLK = 1024
REQS = 64


def draw_queries(key, part):
    key = jax.random.fold_in(key, 7)
    base = jnp.clip(jax.random.normal(key, (2, REQS, H, HD), jnp.float32), -6.0, 6.0)
    return base.astype(jnp.bfloat16)


def place_ends(array, own_key, least, largest):
    shape = array.shape
    place = [jax.random.randint(jax.random.fold_in(own_key, axis), (), 0, shape[axis]) for axis in range(len(shape))]
    array = array.at[tuple(place)].set(least)
    longest = shape.index(max(shape))
    place[longest] = (place[longest] + 1) % shape[longest]
    return array.at[tuple(place)].set(largest)


def block_scale(rng, dims, pieces, smallest, top_value):
    loudness, own = 1.0, jax.random.fold_in(rng, 6)
    for position, blocks in pieces:
        heights = jnp.exp(jax.random.uniform(jax.random.fold_in(own, position), (blocks,), jnp.float32, smallest / len(pieces), top_value / len(pieces)))
        loudness = loudness * jnp.repeat(heights, dims[position] // blocks).reshape([-1 if axis == position else 1 for axis in range(len(dims))])
    return loudness


def length_profile(number_of, total, most, lean):
    loads = [(1 << 20) // math.isqrt(grade ** lean) + 1 for grade in range(2, number_of + 1)]
    rest, given = total - most - (number_of - 1), [1] * (number_of - 1)
    while rest > 0:
        movable = [i for i in range(number_of - 1) if given[i] < most]
        whole, left = sum([loads[i] for i in movable]), rest
        for i in movable:
            more = min(most - given[i], max(1, left * loads[i] // whole), rest)
            given[i] = given[i] + more
            rest = rest - more
    return np.array([most] + given)


def ragged_sizes(key, number_of, total, limit, slope):
    if number_of == 2:
        one = jax.random.randint(key, (), max(1, total - limit), min(limit, total - 1) + 1)
        return jnp.stack([one, total - one])
    tallies = jnp.asarray(length_profile(number_of, total, limit, slope), jnp.int32)
    pairs = (number_of - 1) // 2
    giver, receiver = tallies[1:1 + 2 * pairs:2], tallies[2:2 + 2 * pairs:2]
    slack = jnp.minimum(giver - 1, limit - receiver)
    moved = jax.random.randint(jax.random.fold_in(key, 1), (pairs,), 0, 1 << 20) % (slack + 1)
    tallies = tallies.at[1:1 + 2 * pairs:2].set(giver - moved).at[2:2 + 2 * pairs:2].set(receiver + moved)
    return tallies[jax.random.permutation(jax.random.fold_in(key, 2), number_of)]


def noise(key, shape, scale, limit, cuts=(), held_as=jnp.bfloat16):
    values = scale * jax.random.normal(key, shape, jnp.float32)
    if cuts:
        values = values * block_scale(key, shape, cuts, -0.22, 0.18)
    return jnp.clip(values, -limit, limit).astype(held_as)


def setup_inputs(seed: int = 0) -> dict:
    seeds = jax.random.split(jax.random.key(seed), 8)
    return {
        "kv_pool": noise(seeds[0], (NBLK, KVH, BT, 2 * HD), 1.0, 6.0, ((0, 64), (1, 8))),
        "queries": draw_queries(jax.random.fold_in(seeds[7], 71), 0),
        "new_kv": noise(seeds[2], (2, REQS, KVH, 2 * HD), 1.0, 6.0, ((1, 64), (2, 8))),
        "block_count": ragged_sizes(seeds[3], REQS, NBLK, MAXB, 2).astype(jnp.int32),
        "tail_gap": place_ends(jax.random.randint(seeds[4], (REQS,), 0, BT - 2), jax.random.fold_in(seeds[4], 1), 0, (BT - 2) - 1).astype(jnp.int32),
        "block_place": jax.random.permutation(seeds[5], NBLK).astype(jnp.int32),
        "out_weight": noise(seeds[6], (H * HD, D), (H * HD // BT) ** -0.5, 1.0, ((0, 8), (1, 64))),
    }


masked_value = -1e30


def reference(kv_pool, queries, new_kv, block_count, tail_gap, block_place, out_weight):
    group = H // KVH
    ends = jnp.cumsum(block_count).astype(jnp.int32)
    starts = (ends - block_count).astype(jnp.int32)
    all_places = jnp.arange(NBLK, dtype=jnp.int32)
    rank_of = jnp.zeros((NBLK,), jnp.int32).at[block_place].set(all_places)
    request_of = jnp.sum((ends[None, :] <= rank_of[:, None]).astype(jnp.int32), axis=1)
    block_index = rank_of - starts[request_of]
    context = (block_count * BT - 2 - tail_gap).astype(jnp.int32)
    context_of = context[request_of]
    positions = block_index[:, None] * BT + jnp.arange(BT, dtype=jnp.int32)[None, :]
    cache = kv_pool
    for which in range(2):
        hit = positions == (context_of + which)[:, None]
        rows = new_kv[which][request_of]
        cache = jnp.where(hit[:, None, :, None], rows[:, :, None, :], cache)
    usable = positions[None, :, :] <= (context_of[None, :] + jnp.arange(2, dtype=jnp.int32)[:, None])[:, :, None]
    maxima, sums, outs = [], [], []
    for head_kv in range(KVH):
        keys = cache[:, head_kv, :, :HD].astype(jnp.float32)
        values = cache[:, head_kv, :, HD:].astype(jnp.float32)
        q_rows = queries[:, :, head_kv * group:(head_kv + 1) * group, :][:, request_of].astype(jnp.float32)
        scores = jnp.einsum("sbgd,btd->sbgt", q_rows, keys) * (HD ** -0.5)
        scores = jnp.where(usable[:, :, None, :], scores, masked_value)
        block_max = jnp.max(scores, axis=-1)
        weights = jnp.exp(scores - block_max[..., None])
        maxima.append(block_max)
        sums.append(jnp.sum(weights, axis=-1))
        rounded = weights.astype(jnp.bfloat16).astype(jnp.float32)
        outs.append(jnp.einsum("sbgt,btd->sbgd", rounded, values))
    block_max = jnp.concatenate(maxima, axis=2)
    block_sum = jnp.concatenate(sums, axis=2)
    block_out = jnp.concatenate(outs, axis=2)
    top = jnp.full((2, REQS, H), masked_value, jnp.float32).at[:, request_of, :].max(block_max)
    factor = jnp.exp(block_max - top[:, request_of, :])
    total = jnp.zeros((2, REQS, H), jnp.float32).at[:, request_of, :].add(factor * block_sum)
    combined = jnp.zeros((2, REQS, H, HD), jnp.float32).at[:, request_of].add(factor[..., None] * block_out)
    attended = (combined / total[..., None]).astype(jnp.bfloat16).reshape(2 * REQS, H * HD)
    projected = jnp.dot(attended, out_weight, preferred_element_type=jnp.float32)
    return projected.reshape(2, REQS, D).astype(jnp.bfloat16)
```

```python
import functools

import jax
import jax.numpy as jnp
from jax import lax
from jax.experimental import pallas as pl
from jax.experimental.pallas import tpu as pltpu
from jax.sharding import PartitionSpec as P

MESH = pl.DeviceIdType.MESH
masked_value = -1e30
groups = 4


def iota(shape, axis):
    return lax.broadcasted_iota(jnp.int32, shape, axis).astype(jnp.float32)


def block_tables(bp, cnt, gap, ids, tokens):
    reqs = cnt.shape[1]
    blocks = ids.shape[0]
    rank = jnp.sum(jnp.where(bp == ids, iota((blocks, bp.shape[1]), 1), 0.0), axis=1, keepdims=True)
    row, col = iota((reqs, reqs), 0), iota((reqs, reqs), 1)
    cnt_col = jnp.sum(jnp.where(row == col, cnt, 0.0), axis=1, keepdims=True)
    ends = jnp.sum(jnp.where(row <= col, cnt_col, 0.0), axis=0, keepdims=True)
    request = jnp.sum(jnp.where(ends <= rank, 1.0, 0.0), axis=1, keepdims=True)
    offset = cnt * tokens - 2.0 - gap + (ends - cnt) * tokens
    picked = jnp.sum(
        jnp.where(iota((blocks, reqs), 1) == request, offset, 0.0), axis=1, keepdims=True
    )
    return request, picked - rank * tokens


def kernel(
    X, Z, T,
    q_ref, nk_ref, cnt_ref, gap_ref, bp_ref, kv_hbm, w_hbm, out_ref,
    kv, w, qbuf, obuf, lbuf, oz, lz, ob, lb, abuf, att, ysend, fin,
    sem_in, s1, r1, s2, r2, sa, ra, sal, ral, sb, rb, sbl, rbl, sc, rc, sd, rd, se, re,
):
    pool, ten = lax.axis_index("pool"), lax.axis_index("tensor")
    x, z = lax.div(pool, Z), lax.rem(pool, Z)
    blocks, tokens, hd2 = kv.shape
    hd = hd2 // 2
    rows = q_ref.shape[0]
    reqs = cnt_ref.shape[1]
    per_t = reqs // T
    t_per_x = Z // per_t
    heads = rows // 2
    gs = Z // groups
    scale = hd ** (-0.5)

    def along_z(o):
        return (x * Z + lax.rem(z + o, Z), ten)

    def along_x(o):
        return (lax.rem(x + o, X) * Z + z, ten)

    def loop(low, high, body):
        def step(i, carry):
            body(i)
            return carry

        lax.fori_loop(low, high, step, 0)

    def remote(src, dst, send, recv, device):
        return pltpu.make_async_remote_copy(
            src_ref=src, dst_ref=dst, send_sem=send, recv_sem=recv,
            device_id=device, device_id_type=MESH,
        )

    kv_in = pltpu.make_async_copy(kv_hbm, kv, sem_in.at[0])
    w_in = pltpu.make_async_copy(w_hbm, w, sem_in.at[1])
    kv_in.start()
    w_in.start()

    barrier = pltpu.get_barrier_semaphore()

    def greet(device):
        pl.semaphore_signal(barrier, inc=1, device_id=device, device_id_type=MESH)

    loop(1, Z, lambda o: greet(along_z(o)))
    loop(1, X, lambda o: greet(along_x(o)))
    loop(1, T, lambda o: greet((pool, lax.rem(ten + o, T))))
    qbuf[pool] = q_ref[...]
    pl.semaphore_wait(barrier, Z + X + T - 3)

    def z_copy(buf, s, r, o):
        return remote(buf.at[pool], buf.at[pool], s.at[o], r.at[z], along_z(o))

    def z_arrival(buf, s, r, at):
        here = buf.at[x * Z + at]
        return remote(here, here, s.at[0], r.at[at], along_z(1))

    def x_copy(buf, s, r, g, o):
        part = buf.at[pl.ds(x * Z + g * gs, gs)]
        return remote(part, part, s.at[g, o], r.at[g, x], along_x(o))

    def x_arrival(buf, s, r, g, from_x):
        part = buf.at[pl.ds(from_x * Z + g * gs, gs)]
        return remote(part, part, s.at[g, 0], r.at[g, from_x], along_x(1))

    def gather_z(buf, s, r):
        loop(1, Z, lambda o: z_copy(buf, s, r, o).start())

    def gather_x(buf, sz, rz, sx, rx):
        for turn in (0, 1, 3, 2):
            g = lax.rem(lax.div(z, gs) + turn, groups)

            def arrive(i):
                at = g * gs + i

                @pl.when(at != z)
                def _():
                    z_arrival(buf, sz, rz, at).wait_recv()

            loop(0, gs, arrive)
            loop(1, X, lambda o: x_copy(buf, sx, rx, g, o).start())

    def gathered(buf, sx, rx, from_x):
        loop(0, groups, lambda g: x_arrival(buf, sx, rx, g, from_x).wait_recv())

    def gather_sent(buf, sz, rz, sx, rx):
        loop(1, Z, lambda o: z_copy(buf, sz, rz, o).wait_send())
        loop(0, groups, lambda g: loop(1, X, lambda o: x_copy(buf, sx, rx, g, o).wait_send()))

    gather_z(qbuf, s1, r1)

    cnt = cnt_ref[...].astype(jnp.float32)
    gap = gap_ref[...].astype(jnp.float32)
    line = X * blocks
    b = lax.broadcasted_iota(jnp.int32, (line, 1), 0)
    ids = (lax.rem(x + lax.div(b, blocks), X) * Z + z) * blocks + lax.rem(b, blocks)
    request, usable = block_tables(bp_ref[...], cnt, gap, ids, float(tokens))
    own_request, own_usable = request[:blocks], usable[:blocks]

    own_rows = blocks * rows
    picked_row = (
        jnp.broadcast_to((own_request * rows)[:, None, :], (blocks, rows, 1))
        + iota((blocks, rows, 1), 1)
    ).reshape(own_rows, 1)
    lane = iota((own_rows, Z * rows), 1)

    def pick(j):
        first = lax.rem(x + j, X) * (Z * rows)
        return jnp.where(picked_row - first.astype(jnp.float32) == lane, 1.0, 0.0).astype(
            jnp.bfloat16
        )

    picks = [pick(j) for j in range(X)]

    local = request - (x * Z).astype(jnp.float32)
    line_rows = line * rows
    wide = lax.broadcasted_iota(jnp.int32, (line, line_rows), 1)
    local_lane = jnp.sum(
        jnp.where(
            lax.broadcasted_iota(jnp.int32, (line, line_rows), 0) == lax.div(wide, rows),
            local, 0.0,
        ),
        axis=0, keepdims=True,
    )
    goes_to = local_lane * rows + lax.rem(
        lax.broadcasted_iota(jnp.int32, (1, line_rows), 1), rows
    ).astype(jnp.float32)
    merge = jnp.where(iota((Z * rows, line_rows), 0) == goes_to, 1.0, 0.0).astype(jnp.bfloat16)

    q_own = q_ref[...].astype(jnp.float32)
    new = nk_ref[...].astype(jnp.float32)
    score0 = jnp.sum(q_own * new[0:1, :hd], axis=1, keepdims=True) * scale
    score1 = jnp.sum(q_own * new[1:2, :hd], axis=1, keepdims=True) * scale
    score1 = jnp.where(iota((rows, 1), 0) >= heads, score1, masked_value)
    new_max = jnp.maximum(score0, score1)
    weight0, weight1 = jnp.exp(score0 - new_max), jnp.exp(score1 - new_max)
    new_sum = weight0 + weight1
    new_out = (
        weight0.astype(jnp.bfloat16).astype(jnp.float32) * new[0:1, hd:]
        + weight1.astype(jnp.bfloat16).astype(jnp.float32) * new[1:2, hd:]
    ) / new_sum
    new_lse = new_max + jnp.log(new_sum)

    gather_x(qbuf, s1, r1, s2, r2)

    def dot(a, c):
        return jnp.dot(a, c, preferred_element_type=jnp.float32)

    def column(j):
        from_x = lax.rem(x + j, X)
        if j:
            gathered(qbuf, s2, r2, from_x)
        return qbuf[pl.ds(from_x * Z, Z)].reshape(Z * rows, hd)

    q_sel = dot(picks[0], column(0))
    for j in range(1, X):
        q_sel += dot(picks[j], column(j))
    q_sel = q_sel.astype(jnp.bfloat16).reshape(blocks, rows, hd)

    kv_in.wait()

    def o_copy(c, o):
        part = pl.ds(c * step, step)
        return remote(
            obuf.at[0, part], obuf.at[X - o, part], sa.at[c, o], ra.at[c, X - o], along_x(o)
        )

    def l_copy(o):
        return remote(lbuf.at[0], lbuf.at[X - o], sal.at[o], ral.at[X - o], along_x(o))

    step = blocks // 4
    spread = lax.rem(lax.broadcasted_iota(jnp.int32, (step, rows, 128), 2), rows)
    spread = spread == lax.broadcasted_iota(jnp.int32, (step, rows, 128), 1)
    position = iota((step, rows, tokens), 2)
    lses = []
    for c in range(4):
        part = slice(c * step, (c + 1) * step)
        keys = kv[part, :, :hd]
        values = kv[part, :, hd:]
        scores = jnp.einsum(
            "bqd,btd->bqt", q_sel[part], keys, preferred_element_type=jnp.float32
        ) * scale
        limit = jnp.broadcast_to(own_usable[part][:, None, :], (step, rows, 1))
        scores = jnp.where(position < limit, scores, masked_value)
        top = jnp.max(scores, axis=2, keepdims=True)
        weights = jnp.exp(scores - top)
        total = jnp.sum(weights, axis=2, keepdims=True)
        out = jnp.einsum(
            "bqt,btd->bqd", weights.astype(jnp.bfloat16), values,
            preferred_element_type=jnp.float32,
        )
        obuf[0, part] = (out / total).astype(jnp.bfloat16)
        loop(1, X, lambda o: o_copy(c, o).start())
        lses.append(jnp.sum(jnp.where(spread, top + jnp.log(total), 0.0), axis=1))
    lbuf[0] = jnp.concatenate(lses, axis=0)
    loop(1, X, lambda o: l_copy(o).start())

    for j in range(1, X):
        l_here = lbuf.at[j]
        remote(l_here, l_here, sal.at[0], ral.at[j], along_x(1)).wait_recv()
    lse = lbuf[...].reshape(line, 128)
    where_to = jnp.broadcast_to(local, (line, 128))
    tops = []
    top_of = jnp.zeros((line, 128), jnp.float32)
    for i in range(Z):
        mine = where_to == float(i)
        tops.append(jnp.max(jnp.where(mine, lse, masked_value), axis=0, keepdims=True))
        top_of = jnp.where(mine, tops[i], top_of)
    inside = jnp.logical_and(where_to >= 0.0, where_to < float(Z))
    factor = jnp.where(inside, jnp.exp(jnp.where(inside, lse - top_of, 0.0)), 0.0)
    sum_of = jnp.ones((line, 128), jnp.float32)
    for i in range(Z):
        mine = where_to == float(i)
        total = jnp.sum(jnp.where(mine, factor, 0.0), axis=0, keepdims=True)
        sum_of = jnp.where(mine, total, sum_of)
        lz[i] = jnp.where(
            total > 0.0, tops[i] + jnp.log(jnp.where(total > 0.0, total, 1.0)), masked_value
        )
    factor = factor / sum_of

    def to_column(values, count):
        shape = (count, rows, 128)
        diagonal = lax.broadcasted_iota(jnp.int32, shape, 2) == lax.broadcasted_iota(
            jnp.int32, shape, 1
        )
        return jnp.sum(
            jnp.where(diagonal, jnp.broadcast_to(values, shape), 0.0), axis=2, keepdims=True
        )

    factor = to_column(factor[:, None, :], line)
    for j in range(1, X):
        for c in range(4):
            o_here = obuf.at[j, pl.ds(c * step, step)]
            remote(o_here, o_here, sa.at[c, 0], ra.at[c, j], along_x(1)).wait_recv()
    scaled = (obuf[...].reshape(line, rows, hd).astype(jnp.float32) * factor).reshape(
        line_rows, hd
    )
    high = scaled.astype(jnp.bfloat16)
    low = (scaled - high.astype(jnp.float32)).astype(jnp.bfloat16)
    merged = dot(merge, high) + dot(merge, low)
    oz[...] = merged.astype(jnp.bfloat16).reshape(Z, rows, hd)

    def oz_copy(o):
        to = lax.rem(z + o, Z)
        return remote(oz.at[to], ob.at[Z - o], sb.at[o], rb.at[Z - o], along_z(o))

    def lz_copy(o):
        to = lax.rem(z + o, Z)
        return remote(lz.at[to], lb.at[Z - o], sbl.at[o], rbl.at[Z - o], along_z(o))

    def send_z(o):
        oz_copy(o).start()
        lz_copy(o).start()

    loop(1, Z, send_z)
    ob[0] = oz[z]
    lb[0] = lz[z]

    def arrive_z(o):
        o_here, l_here = ob.at[o], lb.at[o]
        remote(o_here, o_here, sb.at[0], rb.at[o], along_z(1)).wait_recv()
        remote(l_here, l_here, sbl.at[0], rbl.at[o], along_z(1)).wait_recv()

    loop(1, Z, arrive_z)
    lse = to_column(lb[...], Z)
    top = jnp.maximum(jnp.max(lse, axis=0), new_lse)
    factor = jnp.exp(lse - top[None])
    new_factor = jnp.exp(new_lse - top)
    total = jnp.sum(factor, axis=0) + new_factor
    combined = jnp.sum(factor * ob[...].astype(jnp.float32), axis=0) + new_factor * new_out
    abuf[pool] = (combined / total).astype(jnp.bfloat16)

    gather_z(abuf, sc, rc)
    w_in.wait()
    gather_x(abuf, sc, rc, sd, rd)

    def y_copy(j, u, to):
        return remote(
            ysend.at[j, :, pl.ds(u * per_t, per_t)], fin.at[ten], se.at[j, u], re.at[ten],
            (pool, to),
        )

    for j in range(X):
        from_x = lax.rem(x + j, X)
        if j:
            gathered(abuf, sd, rd, from_x)
        att[...] = abuf[pl.ds(from_x * Z, Z)].astype(jnp.float32).reshape(Z * rows, hd)
        steps = []
        for s in range(2):
            parts = [att[pl.ds(s * heads + h, Z, stride=rows), :] for h in range(heads)]
            steps.append(jnp.concatenate(parts, axis=1))
        a = jnp.concatenate(steps, axis=0).astype(jnp.bfloat16)
        ysend[j] = dot(a, w[...]).reshape(2, Z, w.shape[1])
        for u in range(t_per_x):
            to = from_x * t_per_x + u

            @pl.when(to != ten)
            def _():
                y_copy(j, u, to).start()

            @pl.when(to == ten)
            def _():
                fin[ten] = ysend[j, :, u * per_t : (u + 1) * per_t]

    def y_arrive(o):
        at = lax.rem(ten + o, T)
        here = fin.at[at]
        remote(here, here, se.at[0, 0], re.at[at], (pool, at)).wait_recv()

    loop(1, T, y_arrive)
    out_ref[...] = jnp.sum(fin[...], axis=0).astype(jnp.bfloat16)

    gather_sent(qbuf, s1, r1, s2, r2)
    for c in range(4):
        loop(1, X, lambda o: o_copy(c, o).wait_send())
    loop(1, X, lambda o: l_copy(o).wait_send())
    loop(1, Z, lambda o: oz_copy(o).wait_send())
    loop(1, Z, lambda o: lz_copy(o).wait_send())
    gather_sent(abuf, sc, rc, sd, rd)
    for j in range(X):
        for u in range(t_per_x):
            to = lax.rem(x + j, X) * t_per_x + u

            @pl.when(to != ten)
            def _():
                y_copy(j, u, to).wait_send()


def body(X, Z, T, kv_pool, queries, new_kv, block_count, tail_gap, block_place, out_weight):
    blocks, _, tokens, hd2 = kv_pool.shape
    hd = hd2 // 2
    rows = 2 * queries.shape[2]
    reqs = block_count.shape[0]
    columns = out_weight.shape[1]
    pools = X * Z
    dma = pltpu.SemaphoreType.DMA
    in_vmem = pl.BlockSpec(memory_space=pltpu.VMEM)
    in_any = pl.BlockSpec(memory_space=pl.ANY)
    return pl.pallas_call(
        functools.partial(kernel, X, Z, T),
        out_shape=jax.ShapeDtypeStruct((2, reqs // T, columns), jnp.bfloat16),
        in_specs=[in_vmem] * 5 + [in_any] * 2,
        out_specs=in_vmem,
        scratch_shapes=[
            pltpu.VMEM((blocks, tokens, hd2), jnp.bfloat16),
            pltpu.VMEM(out_weight.shape, jnp.bfloat16),
            pltpu.VMEM((pools, rows, hd), jnp.bfloat16),
            pltpu.VMEM((X, blocks, rows, hd), jnp.bfloat16),
            pltpu.VMEM((X, blocks, 128), jnp.float32),
            pltpu.VMEM((Z, rows, hd), jnp.bfloat16),
            pltpu.VMEM((Z, 1, 128), jnp.float32),
            pltpu.VMEM((Z, rows, hd), jnp.bfloat16),
            pltpu.VMEM((Z, 1, 128), jnp.float32),
            pltpu.VMEM((pools, rows, hd), jnp.bfloat16),
            pltpu.VMEM((Z * rows, hd), jnp.float32),
            pltpu.VMEM((X, 2, Z, columns), jnp.float32),
            pltpu.VMEM((T, 2, reqs // T, columns), jnp.float32),
            dma((2,)),
            dma((Z,)), dma((Z,)),
            dma((groups, X)), dma((groups, X)),
            dma((4, X)), dma((4, X)), dma((X,)), dma((X,)),
            dma((Z,)), dma((Z,)), dma((Z,)), dma((Z,)),
            dma((Z,)), dma((Z,)),
            dma((groups, X)), dma((groups, X)),
            dma((X, Z * T // reqs)), dma((T,)),
        ],
        compiler_params=pltpu.CompilerParams(
            collective_id=0, has_side_effects=True, vmem_limit_bytes=40 * 1024 * 1024
        ),
    )(
        queries.reshape(rows, hd),
        new_kv.reshape(2, hd2),
        block_count.reshape(1, reqs),
        tail_gap.reshape(1, reqs),
        block_place.reshape(1, block_place.shape[0]),
        kv_pool.reshape(blocks, tokens, hd2),
        out_weight,
    )


def solution(mesh):
    pools, tensors = mesh.shape["pool"], mesh.shape["tensor"]
    Z = 16 if pools == 64 else 4
    placed = (
        P("pool", "tensor", None, None),
        P(None, "pool", "tensor", None),
        P(None, "pool", "tensor", None),
        P(),
        P(),
        P(),
        P("tensor", "pool"),
    )
    return jax.shard_map(
        functools.partial(body, pools // Z, Z, tensors),
        mesh=mesh, in_specs=placed, out_specs=P(None, "tensor", "pool"), check_vma=False,
    )
```

```python
import functools

import jax
import jax.numpy as jnp
from jax import lax
from jax.experimental import pallas as pl
from jax.experimental.pallas import tpu as pltpu
from jax.sharding import PartitionSpec as P

MESH = pl.DeviceIdType.MESH
masked_value = -1e30
N = 4
chunks = 4


def iota(shape, axis):
    return lax.broadcasted_iota(jnp.int32, shape, axis)


def reals(shape, axis):
    return iota(shape, axis).astype(jnp.float32)


def block_tables(bp, cnt, gap, ids, tokens):
    reqs = cnt.shape[1]
    blocks = ids.shape[0]
    rank = jnp.sum(jnp.where(bp == ids, reals((blocks, bp.shape[1]), 1), 0.0), axis=1, keepdims=True)
    row, col = iota((reqs, reqs), 0), iota((reqs, reqs), 1)
    cnt_col = jnp.sum(jnp.where(row == col, cnt, 0.0), axis=1, keepdims=True)
    ends = jnp.sum(jnp.where(row <= col, cnt_col, 0.0), axis=0, keepdims=True)
    request = jnp.sum(jnp.where(ends <= rank, 1.0, 0.0), axis=1, keepdims=True)
    offset = cnt * tokens - 2.0 - gap + (ends - cnt) * tokens
    picked = jnp.sum(
        jnp.where(reals((blocks, reqs), 1) == request, offset, 0.0), axis=1, keepdims=True
    )
    return request, picked - rank * tokens


def to_column(values, count, rows):
    shape = (count, rows, 128)
    return jnp.sum(
        jnp.where(iota(shape, 2) == iota(shape, 1), jnp.broadcast_to(values, shape), 0.0),
        axis=2, keepdims=True,
    )


def kernel(
    X, Z, T,
    q_hbm, nk_hbm, cnt_hbm, gap_hbm, bp_hbm, kv_hbm, w_hbm, out_ref,
    q_ref, nk_ref, cnt_ref, gap_ref, bp_ref, kv, w,
    qbuf, pick_ref, put_ref, pbuf, lz, rbuf, rl, fb, fl, abuf, att, ysend, fin,
    sem_in, sf, rf, sp, rp, so, ro, sl, rls, sfo, rfo, sfl, rfl, sg, rg, se, re,
):
    pool, ten = lax.axis_index("pool"), lax.axis_index("tensor")
    x, z = lax.div(pool, Z), lax.rem(pool, Z)
    F = Z // N
    G = X * N
    n, f = lax.rem(z, N), lax.div(z, N)
    blocks, tokens, hd2 = kv.shape
    hd = hd2 // 2
    rows = q_ref.shape[0]
    reqs = cnt_ref.shape[1]
    per_t = reqs // T
    t_per_x = Z // per_t
    heads = rows // 2
    scale = hd ** (-0.5)
    frows = F * rows

    xs = [x] + [lax.rem(x + j, X) for j in range(1, X)]
    hops = [0, 1, 2, Z - 1]
    zs = [z] + [lax.rem(z + hops[j], Z) for j in range(1, N)]
    far = [(x * Z + lax.rem(z + N * j, Z), ten) for j in range(F)]
    near = [(xs[g // N] * Z + zs[g % N], ten) for g in range(G)]
    sides = [(pool, lax.rem(ten + j, T)) for j in range(T)]

    def back(g):
        return ((X - g // N) % X) * N + (N - g % N) % N

    order = sorted(range(1, G), key=lambda g: -(min(g // N, X - g // N) + [0, 1, 2, 1][g % N]))

    def remote(src, dst, send, recv, device):
        return pltpu.make_async_remote_copy(
            src_ref=src, dst_ref=dst, send_sem=send, recv_sem=recv,
            device_id=device, device_id_type=MESH,
        )

    def arrived(dst, recv, send):
        remote(dst, dst, send, recv, far[1]).wait_recv()

    pairs = [
        (q_hbm, q_ref), (bp_hbm, bp_ref), (cnt_hbm, cnt_ref), (gap_hbm, gap_ref),
        (nk_hbm, nk_ref), (kv_hbm, kv), (w_hbm, w),
    ]
    loads = [pltpu.make_async_copy(a, b, sem_in.at[i]) for i, (a, b) in enumerate(pairs)]
    for load in loads:
        load.start()

    barrier = pltpu.get_barrier_semaphore()
    for device in far[1:] + near[1:] + sides[1:]:
        pl.semaphore_signal(barrier, inc=1, device_id=device, device_id_type=MESH)
    loads[0].wait()
    qbuf[0, f] = q_ref[...]
    pl.semaphore_wait(barrier, F + G + T - 3)

    def q_far(j):
        return remote(qbuf.at[0, f], qbuf.at[0, f], sf.at[j], rf.at[f], far[j])

    def q_near(g):
        return remote(qbuf.at[0], qbuf.at[back(g)], sp.at[g], rp.at[back(g)], near[g])

    for j in range(1, F):
        q_far(j).start()

    for load in loads[1:5]:
        load.wait()
    cnt = cnt_ref[...].astype(jnp.float32)
    gap = gap_ref[...].astype(jnp.float32)
    ids = pool * blocks + iota((blocks, 1), 0)
    request, usable = block_tables(bp_ref[...], cnt, gap, ids, float(tokens))
    asked = request.astype(jnp.int32)
    asked_x = lax.shift_right_logical(asked, Z.bit_length() - 1)
    slot = (
        jnp.bitwise_and(asked_x - x, X - 1) * N + jnp.bitwise_and(asked - z, N - 1)
    ) * F + lax.shift_right_logical(jnp.bitwise_and(asked, Z - 1), N.bit_length() - 1)

    own_rows = blocks * rows
    all_rows = G * frows
    slot_row = (
        jnp.broadcast_to((slot * rows)[:, None, :], (blocks, rows, 1)) + iota((blocks, rows, 1), 1)
    ).reshape(own_rows, 1)
    half = G * F * rows // X
    for j in range(X):
        pick_ref[j] = jnp.where(slot_row - j * half == iota((own_rows, half), 1), 1.0, 0.0).astype(
            jnp.bfloat16
        )

    q_own = q_ref[...].astype(jnp.float32)
    new = nk_ref[...].astype(jnp.float32)
    score0 = jnp.sum(q_own * new[0:1, :hd], axis=1, keepdims=True) * scale
    score1 = jnp.sum(q_own * new[1:2, :hd], axis=1, keepdims=True) * scale
    score1 = jnp.where(iota((rows, 1), 0) >= heads, score1, masked_value)
    new_max = jnp.maximum(score0, score1)
    weight0, weight1 = jnp.exp(score0 - new_max), jnp.exp(score1 - new_max)
    new_sum = weight0 + weight1
    new_out = (
        weight0.astype(jnp.bfloat16).astype(jnp.float32) * new[0:1, hd:]
        + weight1.astype(jnp.bfloat16).astype(jnp.float32) * new[1:2, hd:]
    ) / new_sum
    lane = iota((rows, 128), 1)
    spread = jnp.bitwise_and(lane, rows - 1) == iota((rows, 128), 0)
    new_lse = jnp.sum(
        jnp.where(spread, new_max + jnp.log(new_sum), 0.0), axis=0, keepdims=True
    )
    rl[G] = jnp.where(lax.div(iota((1, 128), 1), rows) == f, new_lse, masked_value)
    rbuf[G] = jnp.zeros((F, rows, hd), jnp.bfloat16)
    rbuf[G, f] = new_out.astype(jnp.bfloat16)

    for j in range(1, F):
        at = lax.rem(f + j, F)
        arrived(qbuf.at[0, at], rf.at[at], sf.at[0])
    for g in order:
        q_near(g).start()

    slot_lane = jnp.sum(
        jnp.where(
            lax.shift_right_logical(iota((blocks, own_rows), 1), rows.bit_length() - 1)
            == iota((blocks, own_rows), 0),
            slot, 0,
        ).astype(jnp.float32),
        axis=0, keepdims=True,
    )
    goes_to = slot_lane * rows + jnp.bitwise_and(iota((1, own_rows), 1), rows - 1).astype(
        jnp.float32
    )
    for j in range(X):
        put_ref[j] = jnp.where(
            reals((half, own_rows), 0) == goes_to - float(j * half), 1.0, 0.0
        ).astype(jnp.bfloat16)

    def dot(a, c):
        return jnp.dot(a, c, preferred_element_type=jnp.float32)

    def column(j):
        for g in (1, 3, 2) if j == 0 else (0, 1, 3, 2):
            arrived(qbuf.at[j * N + g], rp.at[j * N + g], sp.at[0])
        return dot(pick_ref[j], qbuf[j * N : (j + 1) * N].reshape(half, hd))

    nearest = sorted(range(X), key=lambda j: min(j, X - j))
    q_sel = column(0)
    for j in nearest[1:]:
        q_sel += column(j)
    q_sel = q_sel.astype(jnp.bfloat16).reshape(blocks, rows, hd)

    loads[5].wait()
    step = blocks // chunks
    position = reals((step, rows, tokens), 2)
    outs, lses = [], []
    for c in range(chunks):
        part = slice(c * step, (c + 1) * step)
        scores = jnp.einsum(
            "bqd,btd->bqt", q_sel[part], kv[part, :, :hd], preferred_element_type=jnp.float32
        ) * scale
        limit = jnp.broadcast_to(usable[part][:, None, :], (step, rows, 1))
        scores = jnp.where(position < limit, scores, masked_value)
        top = jnp.max(scores, axis=2, keepdims=True)
        weights = jnp.exp(scores - top)
        total = jnp.sum(weights, axis=2, keepdims=True)
        out = jnp.einsum(
            "bqt,btd->bqd", weights.astype(jnp.bfloat16), kv[part, :, hd:],
            preferred_element_type=jnp.float32,
        )
        outs.append(out / total)
        lses.append(jnp.sum(jnp.where(spread[None], top + jnp.log(total), 0.0), axis=1))
    out = jnp.concatenate(outs, axis=0)
    lse = jnp.concatenate(lses, axis=0)

    def o_copy(g):
        return remote(pbuf.at[g], rbuf.at[back(g)], so.at[g], ro.at[back(g)], near[g])

    def l_copy(g):
        return remote(lz.at[g], rl.at[back(g)], sl.at[g], rls.at[back(g)], near[g])

    wanted = jnp.broadcast_to(request, (blocks, 128))
    best = lse
    for k in range(blocks):
        best = jnp.maximum(
            best, jnp.where(wanted == wanted[k : k + 1], lse[k : k + 1], masked_value)
        )
    factor = jnp.exp(lse - best)
    total = jnp.zeros((blocks, 128), jnp.float32)
    for k in range(blocks):
        total += jnp.where(wanted == wanted[k : k + 1], factor[k : k + 1], 0.0)
    lse = best + jnp.log(total)
    slots = jnp.broadcast_to(slot, (blocks, 128))
    sub = lax.shift_right_logical(iota((blocks, 128), 1), rows.bit_length() - 1)
    for g in order + [0]:
        lz[g] = jnp.max(
            jnp.where(slots - g * F == sub, lse, masked_value), axis=0, keepdims=True
        )
        if g:
            l_copy(g).start()
    scaled = (out * to_column((factor / total)[:, None, :], blocks, rows)).reshape(own_rows, hd)
    high = scaled.astype(jnp.bfloat16)
    low = (scaled - high.astype(jnp.float32)).astype(jnp.bfloat16)
    both = jnp.concatenate([high, low], axis=1)
    for j in nearest[::-1]:
        put = dot(put_ref[j], both)
        pbuf[j * N : (j + 1) * N] = (
            (put[:, :hd] + put[:, hd:]).astype(jnp.bfloat16).reshape(N, F, rows, hd)
        )
        for g in order:
            if g // N == j:
                o_copy(g).start()
    rbuf[0] = pbuf[0]
    rl[0] = lz[0]

    def merged(values, count):
        high = jnp.max(values, axis=0, keepdims=True)
        factor = jnp.exp(values - high)
        total = jnp.sum(factor, axis=0, keepdims=True)
        return to_column(factor / total, count, frows), high + jnp.log(total)

    for g in order:
        arrived(rl.at[g], rls.at[g], sl.at[0])
    share, lse = merged(rl[...], G + 1)
    fl[0] = lse[0]
    acc = jnp.zeros((frows, hd), jnp.float32)
    for g in [G, 0] + order[::-1]:
        if 0 < g < G:
            arrived(rbuf.at[g], ro.at[g], so.at[0])
        acc += share[g] * rbuf[g].astype(jnp.float32).reshape(frows, hd)
    fb[0] = acc.astype(jnp.bfloat16).reshape(F, rows, hd)

    def fo_copy(j):
        return remote(fb.at[0], fb.at[F - j], sfo.at[j], rfo.at[F - j], far[j])

    def fl_copy(j):
        return remote(fl.at[0], fl.at[F - j], sfl.at[j], rfl.at[F - j], far[j])

    for j in range(1, F):
        fl_copy(j).start()
    for j in range(1, F):
        fo_copy(j).start()
    loads[6].wait()
    for j in range(1, F):
        arrived(fl.at[j], rfl.at[j], sfl.at[0])
    share, _ = merged(fl[...], F)
    acc = share[0] * fb[0].astype(jnp.float32).reshape(frows, hd)
    for j in range(1, F):
        arrived(fb.at[j], rfo.at[j], sfo.at[0])
        acc += share[j] * fb[j].astype(jnp.float32).reshape(frows, hd)
    abuf[0] = acc.astype(jnp.bfloat16).reshape(F, rows, hd)

    def a_near(g):
        return remote(abuf.at[0], abuf.at[back(g)], sg.at[g], rg.at[back(g)], near[g])

    for g in order:
        a_near(g).start()

    def y_copy(j, u, to):
        return remote(
            ysend.at[j, :, pl.ds(u * per_t, per_t)], fin.at[ten], se.at[j, u], re.at[ten],
            (pool, to),
        )

    for j in nearest:
        for g in (1, 3, 2) if j == 0 else (0, 1, 3, 2):
            arrived(abuf.at[j * N + g], rg.at[j * N + g], sg.at[0])
        for c in range(N):
            at = j * N + lax.rem(c + N - n, N)
            piece = abuf[at].astype(jnp.float32)
            for i in range(F):
                att[(i * N + c) * rows : (i * N + c + 1) * rows] = piece[i]
        halves = []
        for s in range(2):
            parts = [att[pl.ds(s * heads + h, Z, stride=rows), :] for h in range(heads)]
            halves.append(jnp.concatenate(parts, axis=1))
        a = jnp.concatenate(halves, axis=0).astype(jnp.bfloat16)
        ysend[j] = dot(a, w[...]).reshape(2, Z, w.shape[1])
        for u in range(t_per_x):
            to = xs[j] * t_per_x + u

            @pl.when(to != ten)
            def _():
                y_copy(j, u, to).start()

            @pl.when(to == ten)
            def _():
                fin[ten] = ysend[j, :, u * per_t : (u + 1) * per_t]

    for j in range(1, T):
        at = sides[j][1]
        arrived(fin.at[at], re.at[at], se.at[0, 0])
    out_ref[...] = jnp.sum(fin[...], axis=0).astype(jnp.bfloat16)

    for j in range(1, F):
        q_far(j).wait_send()
        fo_copy(j).wait_send()
        fl_copy(j).wait_send()
    for g in range(1, G):
        q_near(g).wait_send()
        l_copy(g).wait_send()
        o_copy(g).wait_send()
        a_near(g).wait_send()
    for j in range(X):
        for u in range(t_per_x):
            to = xs[j] * t_per_x + u

            @pl.when(to != ten)
            def _():
                y_copy(j, u, to).wait_send()


def body(X, Z, T, kv_pool, queries, new_kv, block_count, tail_gap, block_place, out_weight):
    blocks, _, tokens, hd2 = kv_pool.shape
    hd = hd2 // 2
    rows = 2 * queries.shape[2]
    reqs = block_count.shape[0]
    columns = out_weight.shape[1]
    F, G = Z // N, X * N
    own_rows, half = blocks * rows, N * F * rows
    dma = pltpu.SemaphoreType.DMA
    bf16, f32, i32 = jnp.bfloat16, jnp.float32, jnp.int32
    args = (
        queries.reshape(rows, hd),
        new_kv.reshape(2, hd2),
        block_count.reshape(1, reqs),
        tail_gap.reshape(1, reqs),
        block_place.reshape(1, block_place.shape[0]),
        kv_pool.reshape(blocks, tokens, hd2),
        out_weight,
    )
    return pl.pallas_call(
        functools.partial(kernel, X, Z, T),
        out_shape=jax.ShapeDtypeStruct((2, reqs // T, columns), bf16),
        in_specs=[pl.BlockSpec(memory_space=pl.ANY)] * 7,
        out_specs=pl.BlockSpec(memory_space=pltpu.VMEM),
        scratch_shapes=[pltpu.VMEM(a.shape, a.dtype) for a in args]
        + [
            pltpu.VMEM((G, F, rows, hd), bf16),
            pltpu.VMEM((X, own_rows, half), bf16),
            pltpu.VMEM((X, half, own_rows), bf16),
            pltpu.VMEM((G, F, rows, hd), bf16),
            pltpu.VMEM((G, 1, 128), f32),
            pltpu.VMEM((G + 1, F, rows, hd), bf16),
            pltpu.VMEM((G + 1, 1, 128), f32),
            pltpu.VMEM((F, F, rows, hd), bf16),
            pltpu.VMEM((F, 1, 128), f32),
            pltpu.VMEM((G, F, rows, hd), bf16),
            pltpu.VMEM((Z * rows, hd), f32),
            pltpu.VMEM((X, 2, Z, columns), f32),
            pltpu.VMEM((T, 2, reqs // T, columns), f32),
            dma((7,)),
            dma((F,)), dma((F,)),
            dma((G,)), dma((G,)),
            dma((G,)), dma((G,)), dma((G,)), dma((G,)),
            dma((F,)), dma((F,)), dma((F,)), dma((F,)),
            dma((G,)), dma((G,)),
            dma((X, Z * T // reqs)), dma((T,)),
        ],
        compiler_params=pltpu.CompilerParams(
            collective_id=0, has_side_effects=True, vmem_limit_bytes=60 * 1024 * 1024
        ),
    )(*args)


def solution(mesh):
    pools, tensors = mesh.shape["pool"], mesh.shape["tensor"]
    Z = 16 if pools == 64 else 8
    placed = (
        P("pool", "tensor", None, None),
        P(None, "pool", "tensor", None),
        P(None, "pool", "tensor", None),
        P(),
        P(),
        P(),
        P("tensor", "pool"),
    )
    return jax.shard_map(
        functools.partial(body, pools // Z, Z, tensors),
        mesh=mesh, in_specs=placed, out_specs=P(None, "tensor", "pool"), check_vma=False,
    )
```

```python
import functools

import jax
import jax.numpy as jnp
from jax import lax
from jax.experimental import pallas as pl
from jax.experimental.pallas import tpu as pltpu
from jax.sharding import PartitionSpec as P

MESH = pl.DeviceIdType.MESH
masked_value = -1e30
N = 4
chunks = 4


def iota(shape, axis):
    return lax.broadcasted_iota(jnp.int32, shape, axis)


def reals(shape, axis):
    return iota(shape, axis).astype(jnp.float32)


def block_tables(bp, cnt, gap, ids, tokens):
    reqs = cnt.shape[1]
    blocks = ids.shape[0]
    rank = jnp.sum(jnp.where(bp == ids, reals((blocks, bp.shape[1]), 1), 0.0), axis=1, keepdims=True)
    row, col = iota((reqs, reqs), 0), iota((reqs, reqs), 1)
    cnt_col = jnp.sum(jnp.where(row == col, cnt, 0.0), axis=1, keepdims=True)
    ends = jnp.sum(jnp.where(row <= col, cnt_col, 0.0), axis=0, keepdims=True)
    request = jnp.sum(jnp.where(ends <= rank, 1.0, 0.0), axis=1, keepdims=True)
    offset = cnt * tokens - 2.0 - gap + (ends - cnt) * tokens
    picked = jnp.sum(
        jnp.where(reals((blocks, reqs), 1) == request, offset, 0.0), axis=1, keepdims=True
    )
    return request, picked - rank * tokens


def to_column(values, count, rows):
    shape = (count, rows, 128)
    return jnp.sum(
        jnp.where(iota(shape, 2) == iota(shape, 1), jnp.broadcast_to(values, shape), 0.0),
        axis=2, keepdims=True,
    )


def kernel(
    X, Z, T,
    q_hbm, nk_hbm, cnt_hbm, gap_hbm, bp_hbm, kv_hbm, w_hbm, out_ref,
    nk_ref, cnt_ref, gap_ref, bp_ref, kv, w,
    qbuf, pick_ref, put_ref, pbuf, lz, rbuf, rl, fb, fl, abuf, att, ysend, fin,
    sem_in, sf, rf, sp, rp, so, ro, sl, rls, sfo, rfo, sfl, rfl, sg, rg, se, re,
):
    pool, ten = lax.axis_index("pool"), lax.axis_index("tensor")
    x, z = lax.div(pool, Z), lax.rem(pool, Z)
    F = Z // N
    G = X * N
    n, f = lax.rem(z, N), lax.div(z, N)
    blocks, tokens, hd2 = kv.shape
    hd = hd2 // 2
    rows = q_hbm.shape[0]
    reqs = cnt_ref.shape[1]
    per_t = reqs // T
    t_per_x = Z // per_t
    heads = rows // 2
    scale = hd ** (-0.5)
    frows = F * rows

    xs = [x] + [lax.rem(x + j, X) for j in range(1, X)]
    hops = [[0, 1, 2, Z - 1], [0, 1, Z - 2, Z - 1]]
    zs = {h: z if h == 0 else lax.rem(z + h, Z) for h in set(hops[0] + hops[1])}
    far = [(x * Z + lax.rem(z + N * j, Z), ten) for j in range(F)]
    near = [(xs[g // N] * Z + zs[hops[g // N % 2][g % N]], ten) for g in range(G)]
    sides = [(pool, lax.rem(ten + j, T)) for j in range(T)]

    def back(g):
        return ((X - g // N) % X) * N + (N - g % N) % N

    order = sorted(range(1, G), key=lambda g: -(min(g // N, X - g // N) + [0, 1, 2, 1][g % N]))

    def remote(src, dst, send, recv, device):
        return pltpu.make_async_remote_copy(
            src_ref=src, dst_ref=dst, send_sem=send, recv_sem=recv,
            device_id=device, device_id_type=MESH,
        )

    def arrived(dst, recv, send):
        remote(dst, dst, send, recv, far[1]).wait_recv()

    pairs = [
        (q_hbm, qbuf.at[0, f]), (bp_hbm, bp_ref), (cnt_hbm, cnt_ref), (gap_hbm, gap_ref),
        (nk_hbm, nk_ref), (kv_hbm, kv), (w_hbm, w),
    ]
    loads = [pltpu.make_async_copy(a, b, sem_in.at[i]) for i, (a, b) in enumerate(pairs)]
    barrier = pltpu.get_barrier_semaphore()
    for device in far[1:] + near[1:] + sides[1:]:
        pl.semaphore_signal(barrier, inc=1, device_id=device, device_id_type=MESH)
    for load in loads:
        load.start()
    pl.semaphore_wait(barrier, F + G + T - 3)

    def group(buf, j):
        return buf.at[max(j * N, 1) : (j + 1) * N]

    def group_arrived(buf, recv, send, j):
        here = group(buf, j)
        remote(here, here, send, recv.at[j], far[1]).wait_recv()

    def all_sent(part, send, recv):
        remote(part, part, send, recv, far[1]).wait_send()

    def q_far(j):
        return remote(q_hbm, qbuf.at[0, f], sf.at[j], rf.at[f], far[j])

    def q_near(g):
        return remote(qbuf.at[0], qbuf.at[back(g)], sp.at[0], rp.at[back(g) // N], near[g])

    for j in range(1, F):
        q_far(j).start()

    for load in loads[:5]:
        load.wait()
    cnt = cnt_ref[...].astype(jnp.float32)
    gap = gap_ref[...].astype(jnp.float32)
    ids = pool * blocks + iota((blocks, 1), 0)
    request, usable = block_tables(bp_ref[...], cnt, gap, ids, float(tokens))
    asked = request.astype(jnp.int32)
    asked_x = lax.shift_right_logical(asked, Z.bit_length() - 1)
    slot = (
        jnp.bitwise_and(asked_x - x, X - 1) * N + jnp.bitwise_and(asked - z, N - 1)
    ) * F + lax.shift_right_logical(jnp.bitwise_and(asked, Z - 1), N.bit_length() - 1)

    own_rows = blocks * rows
    all_rows = G * frows
    slot_row = (
        jnp.broadcast_to((slot * rows)[:, None, :], (blocks, rows, 1)) + iota((blocks, rows, 1), 1)
    ).reshape(own_rows, 1)
    half = G * F * rows // X
    for j in range(X):
        pick_ref[j] = jnp.where(slot_row - j * half == iota((own_rows, half), 1), 1.0, 0.0).astype(
            jnp.bfloat16
        )

    q_own = qbuf[0, f].astype(jnp.float32)
    new = nk_ref[...].astype(jnp.float32)
    score0 = jnp.sum(q_own * new[0:1, :hd], axis=1, keepdims=True) * scale
    score1 = jnp.sum(q_own * new[1:2, :hd], axis=1, keepdims=True) * scale
    score1 = jnp.where(iota((rows, 1), 0) >= heads, score1, masked_value)
    new_max = jnp.maximum(score0, score1)
    weight0, weight1 = jnp.exp(score0 - new_max), jnp.exp(score1 - new_max)
    new_sum = weight0 + weight1
    new_out = (
        weight0.astype(jnp.bfloat16).astype(jnp.float32) * new[0:1, hd:]
        + weight1.astype(jnp.bfloat16).astype(jnp.float32) * new[1:2, hd:]
    ) / new_sum
    lane = iota((rows, 128), 1)
    spread = jnp.bitwise_and(lane, rows - 1) == iota((rows, 128), 0)
    new_lse = jnp.sum(
        jnp.where(spread, new_max + jnp.log(new_sum), 0.0), axis=0, keepdims=True
    )
    rl[G] = jnp.where(lax.div(iota((1, 128), 1), rows) == f, new_lse, masked_value)
    rbuf[G] = jnp.zeros((F, rows, hd), jnp.bfloat16)
    rbuf[G, f] = new_out.astype(jnp.bfloat16)

    for j in range(1, F):
        at = lax.rem(f + j, F)
        arrived(qbuf.at[0, at], rf.at[at], sf.at[0])
    for g in order:
        q_near(g).start()

    slot_lane = jnp.sum(
        jnp.where(
            lax.shift_right_logical(iota((blocks, own_rows), 1), rows.bit_length() - 1)
            == iota((blocks, own_rows), 0),
            slot, 0,
        ).astype(jnp.float32),
        axis=0, keepdims=True,
    )
    goes_to = slot_lane * rows + jnp.bitwise_and(iota((1, own_rows), 1), rows - 1).astype(
        jnp.float32
    )
    for j in range(X):
        put_ref[j] = jnp.where(
            reals((half, own_rows), 0) == goes_to - float(j * half), 1.0, 0.0
        ).astype(jnp.bfloat16)

    def dot(a, c):
        return jnp.dot(a, c, preferred_element_type=jnp.float32)

    def column(j):
        group_arrived(qbuf, rp, sp.at[0], j)
        return dot(pick_ref[j], qbuf[j * N : (j + 1) * N].reshape(half, hd))

    nearest = sorted(range(X), key=lambda j: min(j, X - j))
    q_sel = column(0)
    for j in nearest[1:]:
        q_sel += column(j)
    q_sel = q_sel.astype(jnp.bfloat16).reshape(blocks, rows, hd)

    loads[5].wait()
    step = blocks // chunks
    position = reals((step, rows, tokens), 2)
    outs, lses = [], []
    for c in range(chunks):
        part = slice(c * step, (c + 1) * step)
        scores = jnp.einsum(
            "bqd,btd->bqt", q_sel[part], kv[part, :, :hd], preferred_element_type=jnp.float32
        ) * scale
        limit = jnp.broadcast_to(usable[part][:, None, :], (step, rows, 1))
        scores = jnp.where(position < limit, scores, masked_value)
        top = jnp.max(scores, axis=2, keepdims=True)
        weights = jnp.exp(scores - top)
        total = jnp.sum(weights, axis=2, keepdims=True)
        out = jnp.einsum(
            "bqt,btd->bqd", weights.astype(jnp.bfloat16), kv[part, :, hd:],
            preferred_element_type=jnp.float32,
        )
        outs.append(out / total)
        lses.append(jnp.sum(jnp.where(spread[None], top + jnp.log(total), 0.0), axis=1))
    out = jnp.concatenate(outs, axis=0)
    lse = jnp.concatenate(lses, axis=0)

    def o_copy(g):
        return remote(pbuf.at[g], rbuf.at[back(g)], so.at[0], ro.at[back(g) // N], near[g])

    def l_copy(g):
        return remote(lz.at[g], rl.at[back(g)], sl.at[0], rls.at[0], near[g])

    wanted = jnp.broadcast_to(request, (blocks, 128))
    best = lse
    for k in range(blocks):
        best = jnp.maximum(
            best, jnp.where(wanted == wanted[k : k + 1], lse[k : k + 1], masked_value)
        )
    factor = jnp.exp(lse - best)
    total = jnp.zeros((blocks, 128), jnp.float32)
    for k in range(blocks):
        total += jnp.where(wanted == wanted[k : k + 1], factor[k : k + 1], 0.0)
    lse = best + jnp.log(total)
    slots = jnp.broadcast_to(slot, (blocks, 128))
    sub = lax.shift_right_logical(iota((blocks, 128), 1), rows.bit_length() - 1)
    for g in order + [0]:
        lz[g] = jnp.max(
            jnp.where(slots - g * F == sub, lse, masked_value), axis=0, keepdims=True
        )
        if g:
            l_copy(g).start()
    scaled = (out * to_column((factor / total)[:, None, :], blocks, rows)).reshape(own_rows, hd)
    high = scaled.astype(jnp.bfloat16)
    low = (scaled - high.astype(jnp.float32)).astype(jnp.bfloat16)
    both = jnp.concatenate([high, low], axis=1)
    for j in nearest[::-1]:
        put = dot(put_ref[j], both)
        pbuf[j * N : (j + 1) * N] = (
            (put[:, :hd] + put[:, hd:]).astype(jnp.bfloat16).reshape(N, F, rows, hd)
        )
        for g in order:
            if g // N == j:
                o_copy(g).start()
    rbuf[0] = pbuf[0]
    rl[0] = lz[0]

    def merged(values, count):
        high = jnp.max(values, axis=0, keepdims=True)
        factor = jnp.exp(values - high)
        total = jnp.sum(factor, axis=0, keepdims=True)
        return to_column(factor / total, count, frows), high + jnp.log(total)

    arrived(rl.at[1:G], rls.at[0], sl.at[0])
    share, lse = merged(rl[...], G + 1)
    fl[0] = lse[0]
    acc = jnp.zeros((frows, hd), jnp.float32)
    acc += share[G] * rbuf[G].astype(jnp.float32).reshape(frows, hd)
    for j in nearest:
        group_arrived(rbuf, ro, so.at[0], j)
        for g in range(j * N, (j + 1) * N):
            acc += share[g] * rbuf[g].astype(jnp.float32).reshape(frows, hd)
    fb[0] = acc.astype(jnp.bfloat16).reshape(F, rows, hd)

    def fo_copy(j):
        return remote(fb.at[0], fb.at[F - j], sfo.at[j], rfo.at[F - j], far[j])

    def fl_copy(j):
        return remote(fl.at[0], fl.at[F - j], sfl.at[j], rfl.at[F - j], far[j])

    for j in range(1, F):
        fl_copy(j).start()
    for j in range(1, F):
        fo_copy(j).start()
    loads[6].wait()
    for j in range(1, F):
        arrived(fl.at[j], rfl.at[j], sfl.at[0])
    share, _ = merged(fl[...], F)
    acc = share[0] * fb[0].astype(jnp.float32).reshape(frows, hd)
    for j in range(1, F):
        arrived(fb.at[j], rfo.at[j], sfo.at[0])
        acc += share[j] * fb[j].astype(jnp.float32).reshape(frows, hd)
    abuf[0] = acc.astype(jnp.bfloat16).reshape(F, rows, hd)

    def a_near(g):
        return remote(abuf.at[0], abuf.at[back(g)], sg.at[0], rg.at[back(g) // N], near[g])

    for g in order:
        a_near(g).start()

    for j in range(1, F):
        q_far(j).wait_send()
        fo_copy(j).wait_send()
        fl_copy(j).wait_send()
    all_sent(qbuf.at[1:G], sp.at[0], rp.at[0])
    all_sent(lz.at[1:G], sl.at[0], rls.at[0])
    all_sent(pbuf.at[1:G], so.at[0], ro.at[0])

    def y_copy(j, u, to):
        return remote(
            ysend.at[j, :, pl.ds(u * per_t, per_t)], fin.at[lax.rem(ten + T - to, T)],
            se.at[0], re.at[0], (pool, to),
        )

    for j in nearest:
        group_arrived(abuf, rg, sg.at[0], j)
        for c in range(N):
            at = j * N + lax.rem(c + N - n, N)
            piece = abuf[at].astype(jnp.float32)
            for i in range(F):
                att[(i * N + c) * rows : (i * N + c + 1) * rows] = piece[i]
        halves = []
        for s in range(2):
            parts = [att[pl.ds(s * heads + h, Z, stride=rows), :] for h in range(heads)]
            halves.append(jnp.concatenate(parts, axis=1))
        a = jnp.concatenate(halves, axis=0).astype(jnp.bfloat16)
        ysend[j] = dot(a, w[...]).reshape(2, Z, w.shape[1])
        for u in range(t_per_x):
            to = xs[j] * t_per_x + u

            @pl.when(to != ten)
            def _():
                y_copy(j, u, to).start()

            @pl.when(to == ten)
            def _():
                fin[0] = ysend[j, :, u * per_t : (u + 1) * per_t]

    all_sent(abuf.at[1:G], sg.at[0], rg.at[0])
    arrived(fin.at[1:T], re.at[0], se.at[0])
    out_ref[...] = jnp.sum(fin[...], axis=0).astype(jnp.bfloat16)
    all_sent(fin.at[1:T], se.at[0], re.at[0])


def body(X, Z, T, kv_pool, queries, new_kv, block_count, tail_gap, block_place, out_weight):
    blocks, _, tokens, hd2 = kv_pool.shape
    hd = hd2 // 2
    rows = 2 * queries.shape[2]
    reqs = block_count.shape[0]
    columns = out_weight.shape[1]
    F, G = Z // N, X * N
    own_rows, half = blocks * rows, N * F * rows
    dma = pltpu.SemaphoreType.DMA
    bf16, f32, i32 = jnp.bfloat16, jnp.float32, jnp.int32
    args = (
        queries.reshape(rows, hd),
        new_kv.reshape(2, hd2),
        block_count.reshape(1, reqs),
        tail_gap.reshape(1, reqs),
        block_place.reshape(1, block_place.shape[0]),
        kv_pool.reshape(blocks, tokens, hd2),
        out_weight,
    )
    return pl.pallas_call(
        functools.partial(kernel, X, Z, T),
        out_shape=jax.ShapeDtypeStruct((2, reqs // T, columns), bf16),
        in_specs=[pl.BlockSpec(memory_space=pl.ANY)] * 7,
        out_specs=pl.BlockSpec(memory_space=pltpu.VMEM),
        scratch_shapes=[pltpu.VMEM(a.shape, a.dtype) for a in args[1:]]
        + [
            pltpu.VMEM((G, F, rows, hd), bf16),
            pltpu.VMEM((X, own_rows, half), bf16),
            pltpu.VMEM((X, half, own_rows), bf16),
            pltpu.VMEM((G, F, rows, hd), bf16),
            pltpu.VMEM((G, 1, 128), f32),
            pltpu.VMEM((G + 1, F, rows, hd), bf16),
            pltpu.VMEM((G + 1, 1, 128), f32),
            pltpu.VMEM((F, F, rows, hd), bf16),
            pltpu.VMEM((F, 1, 128), f32),
            pltpu.VMEM((G, F, rows, hd), bf16),
            pltpu.VMEM((Z * rows, hd), f32),
            pltpu.VMEM((X, 2, Z, columns), f32),
            pltpu.VMEM((T, 2, reqs // T, columns), f32),
            dma((7,)),
            dma((F,)), dma((F,)),
            dma((1,)), dma((X,)),
            dma((1,)), dma((X,)), dma((1,)), dma((1,)),
            dma((F,)), dma((F,)), dma((F,)), dma((F,)),
            dma((1,)), dma((X,)),
            dma((1,)), dma((1,)),
        ],
        compiler_params=pltpu.CompilerParams(
            collective_id=0, has_side_effects=True, vmem_limit_bytes=60 * 1024 * 1024
        ),
    )(*args)


def solution(mesh):
    pools, tensors = mesh.shape["pool"], mesh.shape["tensor"]
    Z = 16 if pools == 64 else 8
    placed = (
        P("pool", "tensor", None, None),
        P(None, "pool", "tensor", None),
        P(None, "pool", "tensor", None),
        P(),
        P(),
        P(),
        P("tensor", "pool"),
    )
    return jax.shard_map(
        functools.partial(body, pools // Z, Z, tensors),
        mesh=mesh, in_specs=placed, out_specs=P(None, "tensor", "pool"), check_vma=False,
    )
```

```python
import functools

import jax
import jax.numpy as jnp
from jax import lax
from jax.experimental import pallas as pl
from jax.experimental.pallas import tpu as pltpu
from jax.sharding import PartitionSpec as P

MESH = pl.DeviceIdType.MESH
masked_value = -1e30
N = 4
chunks = 2


def iota(shape, axis):
    return lax.broadcasted_iota(jnp.int32, shape, axis)


def reals(shape, axis):
    return iota(shape, axis).astype(jnp.float32)


def block_tables(bp, cnt, gap, ids, tokens):
    reqs = cnt.shape[1]
    blocks = ids.shape[0]
    rank = jnp.sum(jnp.where(bp == ids, reals((blocks, bp.shape[1]), 1), 0.0), axis=1, keepdims=True)
    row, col = iota((reqs, reqs), 0), iota((reqs, reqs), 1)
    cnt_col = jnp.sum(jnp.where(row == col, cnt, 0.0), axis=1, keepdims=True)
    ends = jnp.sum(jnp.where(row <= col, cnt_col, 0.0), axis=0, keepdims=True)
    request = jnp.sum(jnp.where(ends <= rank, 1.0, 0.0), axis=1, keepdims=True)
    offset = cnt * tokens - 2.0 - gap + (ends - cnt) * tokens
    picked = jnp.sum(
        jnp.where(reals((blocks, reqs), 1) == request, offset, 0.0), axis=1, keepdims=True
    )
    return request, picked - rank * tokens


def to_column(values, count, rows):
    shape = (count, rows, 128)
    return jnp.sum(
        jnp.where(iota(shape, 2) == iota(shape, 1), jnp.broadcast_to(values, shape), 0.0),
        axis=2, keepdims=True,
    )


def kernel(
    X, Z, T,
    q_hbm, nk_hbm, cnt_hbm, gap_hbm, bp_hbm, kv_hbm, w_hbm, out_ref,
    nk_ref, cnt_ref, gap_ref, bp_ref, kv, w,
    qbuf, pick_ref, put_ref, slot_ref, goes_ref, limit_ref, qsel_ref, out_blocks, lse_ref, pbuf, lz, rbuf, rl, fb, fl, abuf, att, ysend, fin,
    sem_in, sf, rf, sp, rp, so, ro, sl, rls, sfo, rfo, sfl, rfl, sg, rg, se, re,
):
    pool, ten = lax.axis_index("pool"), lax.axis_index("tensor")
    x, z = lax.div(pool, Z), lax.rem(pool, Z)
    F = Z // N
    G = X * N
    n, f = lax.rem(z, N), lax.div(z, N)
    blocks, tokens, hd2 = kv.shape
    hd = hd2 // 2
    rows = q_hbm.shape[0]
    reqs = cnt_ref.shape[1]
    per_t = reqs // T
    heads = rows // 2
    scale = hd ** (-0.5)
    frows = F * rows

    xs = [x] + [lax.rem(x + j, X) for j in range(1, X)]
    hops = [[0, 1, 2, Z - 1], [0, 1, Z - 2, Z - 1]]
    zs = {h: z if h == 0 else lax.rem(z + h, Z) for h in set(hops[0] + hops[1])}
    far = [(x * Z + lax.rem(z + N * j, Z), ten) for j in range(F)]
    near = [(xs[g // N] * Z + zs[hops[g // N % 2][g % N]], ten) for g in range(G)]
    sides = [(pool, lax.rem(ten + j, T)) for j in range(T)]

    def back(g):
        return ((X - g // N) % X) * N + (N - g % N) % N

    order = sorted(range(1, G), key=lambda g: -(min(g // N, X - g // N) + [0, 1, 2, 1][g % N]))

    def remote(src, dst, send, recv, device):
        return pltpu.make_async_remote_copy(
            src_ref=src, dst_ref=dst, send_sem=send, recv_sem=recv,
            device_id=device, device_id_type=MESH,
        )

    def arrived(dst, recv, send):
        remote(dst, dst, send, recv, far[1]).wait_recv()

    pairs = [
        (q_hbm, qbuf.at[0, f]), (bp_hbm, bp_ref), (cnt_hbm, cnt_ref), (gap_hbm, gap_ref),
        (nk_hbm, nk_ref), (kv_hbm, kv), (w_hbm, w),
    ]
    loads = [pltpu.make_async_copy(a, b, sem_in.at[i]) for i, (a, b) in enumerate(pairs)]
    loads[0].start()
    barrier = pltpu.get_barrier_semaphore()
    for device in far[1:] + near[1:] + sides[1:]:
        pl.semaphore_signal(barrier, inc=1, device_id=device, device_id_type=MESH)
    for load in loads[1:]:
        load.start()
    loads[0].wait()
    pl.semaphore_wait(barrier, F + G + T - 3)

    def group(buf, j):
        if isinstance(j, int):
            return buf.at[max(j * N, 1) : (j + 1) * N]
        return buf.at[pl.ds(j * N, N)]

    fh = F // 2
    parts_f = [pl.ds(0, fh), pl.ds(fh, fh)]
    hrows = fh * rows

    def half_arrived(buf, recv, send, j, p):
        here = group(buf, j).at[:, parts_f[p]]
        remote(here, here, send, recv.at[p * X + j], near[1]).wait_recv()

    def loop(low, high, body):
        def once(i, carry):
            body(i)
            return carry

        lax.fori_loop(low, high, once, 0)

    def group_arrived(buf, recv, send, j):
        here = group(buf, j)
        remote(here, here, send, recv.at[j], far[1]).wait_recv()

    def all_sent(part, send, recv):
        remote(part, part, send, recv, far[1]).wait_send()

    def q_far(j):
        return remote(qbuf.at[0, f], qbuf.at[0, f], sf.at[j], rf.at[f], far[j])

    def q_near(g):
        return remote(qbuf.at[0], qbuf.at[back(g)], sp.at[0], rp.at[back(g) // N], near[g])

    for j in range(1, F):
        q_far(j).start()

    for load in loads[1:5]:
        load.wait()
    cnt = cnt_ref[...].astype(jnp.float32)
    gap = gap_ref[...].astype(jnp.float32)
    ids = pool * blocks + iota((blocks, 1), 0)
    request, usable = block_tables(bp_ref[...], cnt, gap, ids, float(tokens))
    asked = request.astype(jnp.int32)
    asked_x = lax.shift_right_logical(asked, Z.bit_length() - 1)
    slot = (
        jnp.bitwise_and(asked_x - x, X - 1) * N + jnp.bitwise_and(asked - z, N - 1)
    ) * F + lax.shift_right_logical(jnp.bitwise_and(asked, Z - 1), N.bit_length() - 1)

    for b in range(blocks):
        limit_ref[b] = jnp.broadcast_to(usable[b : b + 1], (1, 128))

    own_rows = blocks * rows
    all_rows = G * frows
    slot_row = (
        jnp.broadcast_to((slot * rows)[:, None, :], (blocks, rows, 1)) + iota((blocks, rows, 1), 1)
    ).reshape(own_rows, 1)
    half = G * F * rows // X
    slot_ref[...] = jnp.broadcast_to(slot_row, (own_rows, 128))

    def fill_pick(j):
        here = slot_ref[...][:, :1] - j * half == iota((own_rows, half), 1)
        pick_ref[j] = jnp.where(here, 1.0, 0.0).astype(jnp.bfloat16)

    loop(0, X, fill_pick)

    q_own = qbuf[0, f].astype(jnp.float32)
    new = nk_ref[...].astype(jnp.float32)
    score0 = jnp.sum(q_own * new[0:1, :hd], axis=1, keepdims=True) * scale
    score1 = jnp.sum(q_own * new[1:2, :hd], axis=1, keepdims=True) * scale
    score1 = jnp.where(iota((rows, 1), 0) >= heads, score1, masked_value)
    new_max = jnp.maximum(score0, score1)
    weight0, weight1 = jnp.exp(score0 - new_max), jnp.exp(score1 - new_max)
    new_sum = weight0 + weight1
    new_out = (
        weight0.astype(jnp.bfloat16).astype(jnp.float32) * new[0:1, hd:]
        + weight1.astype(jnp.bfloat16).astype(jnp.float32) * new[1:2, hd:]
    ) / new_sum
    lane = iota((rows, 128), 1)
    spread = jnp.bitwise_and(lane, rows - 1) == iota((rows, 128), 0)
    new_lse = jnp.sum(
        jnp.where(spread, new_max + jnp.log(new_sum), 0.0), axis=0, keepdims=True
    )
    rl[G] = jnp.where(lax.div(iota((1, 128), 1), rows) == f, new_lse, masked_value)
    rbuf[G] = jnp.zeros((F, rows, hd), jnp.bfloat16)
    rbuf[G, f] = new_out.astype(jnp.bfloat16)

    for j in range(1, F):
        at = lax.rem(f + j, F)
        arrived(qbuf.at[0, at], rf.at[at], sf.at[0])
    for g in order:
        q_near(g).start()

    slot_lane = jnp.sum(
        jnp.where(
            lax.shift_right_logical(iota((blocks, own_rows), 1), rows.bit_length() - 1)
            == iota((blocks, own_rows), 0),
            slot, 0,
        ).astype(jnp.float32),
        axis=0, keepdims=True,
    )
    goes_to = slot_lane * rows + jnp.bitwise_and(iota((1, own_rows), 1), rows - 1).astype(
        jnp.float32
    )
    goes_ref[...] = goes_to

    row = iota((N * hrows, own_rows), 0)
    row = (row + lax.shift_right_logical(row, hrows.bit_length() - 1) * hrows).astype(jnp.float32)

    def fill_put(i):
        first = lax.rem(i, X) * half + lax.div(i, X) * hrows
        here = goes_ref[...] - first.astype(jnp.float32) == row
        put_ref[i] = jnp.where(here, 1.0, 0.0).astype(jnp.bfloat16)

    loop(0, 2 * X, fill_put)

    def dot(a, c):
        return jnp.dot(a, c, preferred_element_type=jnp.float32)

    def column(j):
        group_arrived(qbuf, rp, sp.at[0], j)
        return dot(pick_ref[j], qbuf[j * N : (j + 1) * N].reshape(half, hd))

    nearest = sorted(range(X), key=lambda j: min(j, X - j))
    q_sel = column(0)
    for j in nearest[1:]:
        q_sel += column(j)
    qsel_ref[...] = q_sel.astype(jnp.bfloat16).reshape(blocks, rows, hd)

    loads[5].wait()
    step = blocks // chunks
    position = reals((step, rows, tokens), 2)

    def attend(c):
        part = pl.ds(c * step, step)
        scores = jnp.einsum(
            "bqd,btd->bqt", qsel_ref[part], kv[part, :, :hd], preferred_element_type=jnp.float32
        ) * scale
        limit = jnp.broadcast_to(limit_ref[part], (step, 1, 128))
        limit = jnp.concatenate([limit] * (tokens // 128), axis=2)
        scores = jnp.where(position < limit, scores, masked_value)
        top = jnp.max(scores, axis=2, keepdims=True)
        weights = jnp.exp(scores - top)
        total = jnp.sum(weights, axis=2, keepdims=True)
        out = jnp.einsum(
            "bqt,btd->bqd", weights.astype(jnp.bfloat16), kv[part, :, hd:],
            preferred_element_type=jnp.float32,
        )
        out_blocks[part] = out / total
        lse_ref[c] = jnp.sum(jnp.where(spread[None], top + jnp.log(total), 0.0), axis=1)

    loop(0, chunks, attend)
    out = out_blocks[...]
    lse = lse_ref[...].reshape(blocks, 128)

    def o_copy(g, p):
        part = parts_f[p]
        return remote(
            pbuf.at[g, part], rbuf.at[back(g), part], so.at[0], ro.at[p * X + back(g) // N], near[g]
        )

    def l_copy(g):
        return remote(lz.at[g], rl.at[back(g)], sl.at[0], rls.at[0], near[g])

    wanted = jnp.broadcast_to(request, (blocks, 128))
    best = lse
    for k in range(blocks):
        best = jnp.maximum(
            best, jnp.where(wanted == wanted[k : k + 1], lse[k : k + 1], masked_value)
        )
    factor = jnp.exp(lse - best)
    total = jnp.zeros((blocks, 128), jnp.float32)
    for k in range(blocks):
        total += jnp.where(wanted == wanted[k : k + 1], factor[k : k + 1], 0.0)
    lse = best + jnp.log(total)
    slots = jnp.broadcast_to(slot, (blocks, 128))
    sub = lax.shift_right_logical(iota((blocks, 128), 1), rows.bit_length() - 1)
    scaled = (out * to_column((factor / total)[:, None, :], blocks, rows)).reshape(own_rows, hd)
    high = scaled.astype(jnp.bfloat16)
    low = (scaled - high.astype(jnp.float32)).astype(jnp.bfloat16)
    both = jnp.concatenate([high, low], axis=1)
    for i, (p, j) in enumerate([(p, j) for p in range(2) for j in nearest[::-1]]):
        put = dot(put_ref[p * X + j], both)
        put = (put[:, :hd] + put[:, hd:]).astype(jnp.bfloat16)
        pbuf[j * N : (j + 1) * N, p * fh : (p + 1) * fh] = put.reshape(N, fh, rows, hd)
        for g in order:
            if g // N == j:
                o_copy(g, p).start()
        if i == 0:
            for g in order + [0]:
                lz[g] = jnp.max(
                    jnp.where(slots - g * F == sub, lse, masked_value), axis=0, keepdims=True
                )
                if g:
                    l_copy(g).start()
    rbuf[0] = pbuf[0]
    rl[0] = lz[0]

    def merged(values, count):
        high = jnp.max(values, axis=0, keepdims=True)
        factor = jnp.exp(values - high)
        total = jnp.sum(factor, axis=0, keepdims=True)
        return to_column(factor / total, count, frows), high + jnp.log(total)

    arrived(rl.at[1:G], rls.at[0], sl.at[0])
    share, lse = merged(rl[...], G + 1)
    fl[0] = lse[0]

    def fo_copy(j, p):
        part = parts_f[p]
        return remote(
            fb.at[0, part], fb.at[F - j, part], sfo.at[p * F + j], rfo.at[p * F + F - j], far[j]
        )

    def fl_copy(j):
        return remote(fl.at[0], fl.at[F - j], sfl.at[j], rfl.at[F - j], far[j])

    def weighted(share, buf, g, p):
        here = buf[g, p * fh : (p + 1) * fh].astype(jnp.float32).reshape(hrows, hd)
        return share[g][p * hrows : (p + 1) * hrows] * here

    def stored(acc):
        return acc.astype(jnp.bfloat16).reshape(fh, rows, hd)

    for j in range(1, F):
        fl_copy(j).start()
    for p in range(2):
        acc = weighted(share, rbuf, G, p)
        for j in nearest:
            half_arrived(rbuf, ro, so.at[0], j, p)
            for g in range(j * N, (j + 1) * N):
                acc += weighted(share, rbuf, g, p)
        fb[0, p * fh : (p + 1) * fh] = stored(acc)
        for j in range(1, F):
            fo_copy(j, p).start()
    loads[6].wait()
    for j in range(1, F):
        arrived(fl.at[j], rfl.at[j], sfl.at[0])
    share, _ = merged(fl[...], F)

    def a_near(g, p):
        part = parts_f[p]
        return remote(
            abuf.at[0, part], abuf.at[back(g), part], sg.at[0], rg.at[p * X + back(g) // N], near[g]
        )

    for p in range(2):
        acc = weighted(share, fb, 0, p)
        for j in range(1, F):
            here = fb.at[j, parts_f[p]]
            arrived(here, rfo.at[p * F + j], sfo.at[0])
            acc += weighted(share, fb, j, p)
        abuf[0, p * fh : (p + 1) * fh] = stored(acc)
        for g in order:
            a_near(g, p).start()

    for j in range(1, F):
        q_far(j).wait_send()
        fo_copy(j, 0).wait_send()
        fo_copy(j, 1).wait_send()
        fl_copy(j).wait_send()
    all_sent(qbuf.at[1:G], sp.at[0], rp.at[0])
    all_sent(lz.at[1:G], sl.at[0], rls.at[0])
    all_sent(pbuf.at[1:G], so.at[0], ro.at[0])

    def y_copy(j, p, to):
        return remote(
            ysend.at[p, j], fin.at[lax.rem(ten + T - to, T)], se.at[0], re.at[0], (pool, to)
        )

    def project(j, p):
        half_arrived(abuf, rg, sg.at[0], j, p)
        for c in range(N):
            at = j * N + lax.rem(c + N - n, N)
            piece = abuf[at, p * fh : (p + 1) * fh].astype(jnp.float32)
            for i in range(fh):
                att[(i * N + c) * rows : (i * N + c + 1) * rows] = piece[i]
        halves = []
        for s in range(2):
            parts = [att[pl.ds(s * heads + h, per_t, stride=rows), :] for h in range(heads)]
            halves.append(jnp.concatenate(parts, axis=1))
        a = jnp.concatenate(halves, axis=0).astype(jnp.bfloat16)
        ysend[p, j] = dot(a, w[...]).reshape(2, per_t, w.shape[1])
        to = lax.rem(x + j, X) * 2 + p

        @pl.when(to != ten)
        def _():
            y_copy(j, p, to).start()

        @pl.when(to == ten)
        def _():
            fin[0] = ysend[p, j]

    for p in range(2):
        project(0, p)
        loop(1, X, lambda i: project(i + lax.div(i, 2) * (1 - 2 * lax.rem(i, 2)), p))
    all_sent(abuf.at[1:G], sg.at[0], rg.at[0])
    arrived(fin.at[1:T], re.at[0], se.at[0])
    out_ref[...] = jnp.sum(fin[...], axis=0).astype(jnp.bfloat16)
    all_sent(fin.at[1:T], se.at[0], re.at[0])


def body(X, Z, T, kv_pool, queries, new_kv, block_count, tail_gap, block_place, out_weight):
    blocks, _, tokens, hd2 = kv_pool.shape
    hd = hd2 // 2
    rows = 2 * queries.shape[2]
    reqs = block_count.shape[0]
    columns = out_weight.shape[1]
    F, G = Z // N, X * N
    own_rows, half = blocks * rows, N * F * rows
    dma = pltpu.SemaphoreType.DMA
    bf16, f32, i32 = jnp.bfloat16, jnp.float32, jnp.int32
    args = (
        queries.reshape(rows, hd),
        new_kv.reshape(2, hd2),
        block_count.reshape(1, reqs),
        tail_gap.reshape(1, reqs),
        block_place.reshape(1, block_place.shape[0]),
        kv_pool.reshape(blocks, tokens, hd2),
        out_weight,
    )
    return pl.pallas_call(
        functools.partial(kernel, X, Z, T),
        out_shape=jax.ShapeDtypeStruct((2, reqs // T, columns), bf16),
        in_specs=[pl.BlockSpec(memory_space=pl.ANY)] * 7,
        out_specs=pl.BlockSpec(memory_space=pltpu.VMEM),
        scratch_shapes=[pltpu.VMEM(a.shape, a.dtype) for a in args[1:]]
        + [
            pltpu.VMEM((G, F, rows, hd), bf16),
            pltpu.VMEM((X, own_rows, half), bf16),
            pltpu.VMEM((2 * X, half // 2, own_rows), bf16),
            pltpu.VMEM((own_rows, 128), i32),
            pltpu.VMEM((1, own_rows), f32),
            pltpu.VMEM((blocks, 1, 128), f32),
            pltpu.VMEM((blocks, rows, hd), bf16),
            pltpu.VMEM((blocks, rows, hd), f32),
            pltpu.VMEM((chunks, blocks // chunks, 128), f32),
            pltpu.VMEM((G, F, rows, hd), bf16),
            pltpu.VMEM((G, 1, 128), f32),
            pltpu.VMEM((G + 1, F, rows, hd), bf16),
            pltpu.VMEM((G + 1, 1, 128), f32),
            pltpu.VMEM((F, F, rows, hd), bf16),
            pltpu.VMEM((F, 1, 128), f32),
            pltpu.VMEM((G, F, rows, hd), bf16),
            pltpu.VMEM((Z * rows // 2, hd), f32),
            pltpu.VMEM((2, X, 2, reqs // T, columns), f32),
            pltpu.VMEM((T, 2, reqs // T, columns), f32),
            dma((7,)),
            dma((F,)), dma((F,)),
            dma((1,)), dma((X,)),
            dma((1,)), dma((2 * X,)), dma((1,)), dma((1,)),
            dma((2 * F,)), dma((2 * F,)), dma((F,)), dma((F,)),
            dma((1,)), dma((2 * X,)),
            dma((1,)), dma((1,)),
        ],
        compiler_params=pltpu.CompilerParams(
            collective_id=0, has_side_effects=True, vmem_limit_bytes=40 * 1024 * 1024
        ),
    )(*[pltpu.with_memory_space_constraint(a, pltpu.HBM) for a in args])


def solution(mesh):
    pools, tensors = mesh.shape["pool"], mesh.shape["tensor"]
    Z = 16
    placed = (
        P("pool", "tensor", None, None),
        P(None, "pool", "tensor", None),
        P(None, "pool", "tensor", None),
        P(),
        P(),
        P(),
        P("tensor", "pool"),
    )
    return jax.shard_map(
        functools.partial(body, pools // Z, Z, tensors),
        mesh=mesh, in_specs=placed, out_specs=P(None, "tensor", "pool"), check_vma=False,
    )
```

```python
import functools

import jax
import jax.numpy as jnp
from jax import lax
from jax.experimental import pallas as pl
from jax.experimental.pallas import tpu as pltpu
from jax.sharding import PartitionSpec as P

MESH = pl.DeviceIdType.MESH
masked_value = -1e30
N = 4
chunks = 2


def iota(shape, axis):
    return lax.broadcasted_iota(jnp.int32, shape, axis)


def reals(shape, axis):
    return iota(shape, axis).astype(jnp.float32)


def block_tables(bp, cnt, gap, ids, tokens):
    reqs = cnt.shape[1]
    blocks = ids.shape[0]
    rank = jnp.sum(jnp.where(bp == ids, reals((blocks, bp.shape[1]), 1), 0.0), axis=1, keepdims=True)
    row, col = iota((reqs, reqs), 0), iota((reqs, reqs), 1)
    cnt_col = jnp.sum(jnp.where(row == col, cnt, 0.0), axis=1, keepdims=True)
    ends = jnp.sum(jnp.where(row <= col, cnt_col, 0.0), axis=0, keepdims=True)
    request = jnp.sum(jnp.where(ends <= rank, 1.0, 0.0), axis=1, keepdims=True)
    offset = cnt * tokens - 2.0 - gap + (ends - cnt) * tokens
    picked = jnp.sum(
        jnp.where(reals((blocks, reqs), 1) == request, offset, 0.0), axis=1, keepdims=True
    )
    return request, picked - rank * tokens


def to_column(values, count, rows):
    shape = (count, rows, 128)
    return jnp.sum(
        jnp.where(iota(shape, 2) == iota(shape, 1), jnp.broadcast_to(values, shape), 0.0),
        axis=2, keepdims=True,
    )


def in_three(values, rows):
    high = values.astype(jnp.bfloat16).astype(jnp.float32)
    middle = (values - high).astype(jnp.bfloat16).astype(jnp.float32)
    low = values - high - middle
    row = iota((rows, 128), 0)
    tile = jnp.where(row == 0, high, jnp.where(row == 1, middle, jnp.where(row == 2, low, 0.0)))
    return tile.astype(jnp.bfloat16)


def kernel(
    X, Z, T,
    q_hbm, nk_hbm, cnt_hbm, gap_hbm, bp_hbm, kv_hbm, w_hbm, out_ref,
    nk_ref, cnt_ref, gap_ref, bp_ref, kv, w,
    qbuf, pick_ref, put_ref, slot_ref, goes_ref, limit_ref, qsel_ref, out_blocks, lse_ref, pbuf, rbuf, fb, abuf, att, ysend, fin,
    sem_in, sf, rf, sp, rp, so, ro, sfo, rfo, sg, rg, se, re,
):
    pool, ten = lax.axis_index("pool"), lax.axis_index("tensor")
    x, z = lax.div(pool, Z), lax.rem(pool, Z)
    F = Z // N
    G = X * N
    n, f = lax.rem(z, N), lax.div(z, N)
    blocks, tokens, hd2 = kv.shape
    hd = hd2 // 2
    rows = q_hbm.shape[0]
    reqs = cnt_ref.shape[1]
    per_t = reqs // T
    t_per_x = Z // per_t
    heads = rows // 2
    scale = hd ** (-0.5)
    frows = F * rows

    xs = [x] + [lax.rem(x + j, X) for j in range(1, X)]
    hops = [[0, 1, 2, Z - 1], [0, 1, Z - 2, Z - 1]]
    zs = {h: z if h == 0 else lax.rem(z + h, Z) for h in set(hops[0] + hops[1])}
    far = [(x * Z + lax.rem(z + N * j, Z), ten) for j in range(F)]
    near = [(xs[g // N] * Z + zs[hops[g // N % 2][g % N]], ten) for g in range(G)]
    sides = [(pool, lax.rem(ten + j, T)) for j in range(T)]

    def back(g):
        return ((X - g // N) % X) * N + (N - g % N) % N

    order = sorted(range(1, G), key=lambda g: -(min(g // N, X - g // N) + [0, 1, 2, 1][g % N]))

    def remote(src, dst, send, recv, device):
        return pltpu.make_async_remote_copy(
            src_ref=src, dst_ref=dst, send_sem=send, recv_sem=recv,
            device_id=device, device_id_type=MESH,
        )

    def arrived(dst, recv, send):
        remote(dst, dst, send, recv, far[1]).wait_recv()

    pairs = [
        (q_hbm, qbuf.at[0, f]), (bp_hbm, bp_ref), (cnt_hbm, cnt_ref), (gap_hbm, gap_ref),
        (nk_hbm, nk_ref), (kv_hbm, kv), (w_hbm, w),
    ]
    loads = [pltpu.make_async_copy(a, b, sem_in.at[i]) for i, (a, b) in enumerate(pairs)]
    loads[0].start()
    barrier = pltpu.get_barrier_semaphore()
    for device in far[1:] + near[1:] + sides[1:]:
        pl.semaphore_signal(barrier, inc=1, device_id=device, device_id_type=MESH)
    for load in loads[1:]:
        load.start()
    loads[0].wait()
    pl.semaphore_wait(barrier, F + G + T - 3)

    def group(buf, j):
        if isinstance(j, int):
            return buf.at[max(j * N, 1) : (j + 1) * N]
        return buf.at[pl.ds(j * N, N)]

    def loop(low, high, body):
        def once(i, carry):
            body(i)
            return carry

        lax.fori_loop(low, high, once, 0)

    def group_arrived(buf, recv, send, j):
        here = group(buf, j)
        remote(here, here, send, recv.at[j], far[1]).wait_recv()

    def all_sent(part, send, recv):
        remote(part, part, send, recv, far[1]).wait_send()

    def q_far(j):
        return remote(qbuf.at[0, f], qbuf.at[0, f], sf.at[j], rf.at[f], far[j])

    def q_near(g):
        return remote(qbuf.at[0], qbuf.at[back(g)], sp.at[0], rp.at[back(g) // N], near[g])

    for j in range(1, F):
        q_far(j).start()

    for load in loads[1:5]:
        load.wait()
    cnt = cnt_ref[...].astype(jnp.float32)
    gap = gap_ref[...].astype(jnp.float32)
    ids = pool * blocks + iota((blocks, 1), 0)
    request, usable = block_tables(bp_ref[...], cnt, gap, ids, float(tokens))
    asked = request.astype(jnp.int32)
    asked_x = lax.shift_right_logical(asked, Z.bit_length() - 1)
    slot = (
        jnp.bitwise_and(asked_x - x, X - 1) * N + jnp.bitwise_and(asked - z, N - 1)
    ) * F + lax.shift_right_logical(jnp.bitwise_and(asked, Z - 1), N.bit_length() - 1)

    for b in range(blocks):
        limit_ref[b] = jnp.broadcast_to(usable[b : b + 1], (1, 128))

    own_rows = blocks * rows
    all_rows = G * frows
    slot_row = (
        jnp.broadcast_to((slot * rows)[:, None, :], (blocks, rows, 1)) + iota((blocks, rows, 1), 1)
    ).reshape(own_rows, 1)
    half = G * F * rows // X
    slot_ref[...] = jnp.broadcast_to(slot_row, (own_rows, 128))

    def fill_pick(j):
        here = slot_ref[...][:, :1] - j * half == iota((own_rows, half), 1)
        pick_ref[j] = jnp.where(here, 1.0, 0.0).astype(jnp.bfloat16)

    loop(0, X, fill_pick)

    q_own = qbuf[0, f].astype(jnp.float32)
    new = nk_ref[...].astype(jnp.float32)
    score0 = jnp.sum(q_own * new[0:1, :hd], axis=1, keepdims=True) * scale
    score1 = jnp.sum(q_own * new[1:2, :hd], axis=1, keepdims=True) * scale
    score1 = jnp.where(iota((rows, 1), 0) >= heads, score1, masked_value)
    new_max = jnp.maximum(score0, score1)
    weight0, weight1 = jnp.exp(score0 - new_max), jnp.exp(score1 - new_max)
    new_sum = weight0 + weight1
    new_out = (
        weight0.astype(jnp.bfloat16).astype(jnp.float32) * new[0:1, hd:]
        + weight1.astype(jnp.bfloat16).astype(jnp.float32) * new[1:2, hd:]
    ) / new_sum
    lane = iota((rows, 128), 1)
    spread = jnp.bitwise_and(lane, rows - 1) == iota((rows, 128), 0)
    new_lse = jnp.sum(
        jnp.where(spread, new_max + jnp.log(new_sum), 0.0), axis=0, keepdims=True
    )
    rbuf[G] = jnp.zeros((F + 1, rows, hd), jnp.bfloat16)
    new_lse = jnp.where(lax.div(iota((1, 128), 1), rows) == f, new_lse, masked_value)
    rbuf[G, F] = in_three(new_lse, rows)
    rbuf[G, f] = new_out.astype(jnp.bfloat16)

    for j in range(1, F):
        at = lax.rem(f + j, F)
        arrived(qbuf.at[0, at], rf.at[at], sf.at[0])
    for g in order:
        q_near(g).start()

    slot_lane = jnp.sum(
        jnp.where(
            lax.shift_right_logical(iota((blocks, own_rows), 1), rows.bit_length() - 1)
            == iota((blocks, own_rows), 0),
            slot, 0,
        ).astype(jnp.float32),
        axis=0, keepdims=True,
    )
    goes_to = slot_lane * rows + jnp.bitwise_and(iota((1, own_rows), 1), rows - 1).astype(
        jnp.float32
    )
    goes_ref[...] = goes_to

    def fill_put(j):
        here = goes_ref[...] - (j * half).astype(jnp.float32) == reals((half, own_rows), 0)
        put_ref[j] = jnp.where(here, 1.0, 0.0).astype(jnp.bfloat16)

    loop(0, X, fill_put)

    def dot(a, c):
        return jnp.dot(a, c, preferred_element_type=jnp.float32)

    def column(j):
        group_arrived(qbuf, rp, sp.at[0], j)
        return dot(pick_ref[j], qbuf[j * N : (j + 1) * N].reshape(half, hd))

    nearest = sorted(range(X), key=lambda j: min(j, X - j))
    q_sel = column(0)
    for j in nearest[1:]:
        q_sel += column(j)
    qsel_ref[...] = q_sel.astype(jnp.bfloat16).reshape(blocks, rows, hd)

    loads[5].wait()
    step = blocks // chunks
    position = reals((step, rows, tokens), 2)

    def attend(c):
        part = pl.ds(c * step, step)
        scores = jnp.einsum(
            "bqd,btd->bqt", qsel_ref[part], kv[part, :, :hd], preferred_element_type=jnp.float32
        ) * scale
        limit = jnp.broadcast_to(limit_ref[part], (step, 1, 128))
        limit = jnp.concatenate([limit] * (tokens // 128), axis=2)
        scores = jnp.where(position < limit, scores, masked_value)
        top = jnp.max(scores, axis=2, keepdims=True)
        weights = jnp.exp(scores - top)
        total = jnp.sum(weights, axis=2, keepdims=True)
        out = jnp.einsum(
            "bqt,btd->bqd", weights.astype(jnp.bfloat16), kv[part, :, hd:],
            preferred_element_type=jnp.float32,
        )
        out_blocks[part] = out / total
        lse_ref[c] = jnp.sum(jnp.where(spread[None], top + jnp.log(total), 0.0), axis=1)

    loop(0, chunks, attend)
    out = out_blocks[...]
    lse = lse_ref[...].reshape(blocks, 128)

    def o_copy(g):
        return remote(pbuf.at[g], rbuf.at[back(g)], so.at[0], ro.at[back(g) // N], near[g])

    wanted = jnp.broadcast_to(request, (blocks, 128))
    best = lse
    for k in range(blocks):
        best = jnp.maximum(
            best, jnp.where(wanted == wanted[k : k + 1], lse[k : k + 1], masked_value)
        )
    factor = jnp.exp(lse - best)
    total = jnp.zeros((blocks, 128), jnp.float32)
    for k in range(blocks):
        total += jnp.where(wanted == wanted[k : k + 1], factor[k : k + 1], 0.0)
    lse = best + jnp.log(total)
    slots = jnp.broadcast_to(slot, (blocks, 128))
    sub = lax.shift_right_logical(iota((blocks, 128), 1), rows.bit_length() - 1)
    for g in order + [0]:
        row = jnp.max(jnp.where(slots - g * F == sub, lse, masked_value), axis=0, keepdims=True)
        pbuf[g, F] = in_three(row, rows)
    scaled = (out * to_column((factor / total)[:, None, :], blocks, rows)).reshape(own_rows, hd)
    high = scaled.astype(jnp.bfloat16)
    low = (scaled - high.astype(jnp.float32)).astype(jnp.bfloat16)
    both = jnp.concatenate([high, low], axis=1)
    for j in nearest[::-1]:
        put = dot(put_ref[j], both)
        pbuf[j * N : (j + 1) * N, :F] = (
            (put[:, :hd] + put[:, hd:]).astype(jnp.bfloat16).reshape(N, F, rows, hd)
        )
        for g in order:
            if g // N == j:
                o_copy(g).start()
    rbuf[0] = pbuf[0]

    def merged(buf, count):
        values = jnp.sum(buf[:, F].astype(jnp.float32), axis=1, keepdims=True)
        high = jnp.max(values, axis=0, keepdims=True)
        factor = jnp.exp(values - high)
        total = jnp.sum(factor, axis=0, keepdims=True)
        share = to_column(factor / total, count, frows)
        acc = share[0] * buf[0, :F].astype(jnp.float32).reshape(frows, hd)
        for g in range(1, count):
            acc += share[g] * buf[g, :F].astype(jnp.float32).reshape(frows, hd)
        return acc.astype(jnp.bfloat16).reshape(F, rows, hd), high[0] + jnp.log(total[0])

    for j in nearest:
        group_arrived(rbuf, ro, so.at[0], j)
    out, lse = merged(rbuf, G + 1)
    fb[0, :F] = out
    fb[0, F] = in_three(lse, rows)

    def fo_copy(j):
        return remote(fb.at[0], fb.at[F - j], sfo.at[j], rfo.at[F - j], far[j])

    for j in range(1, F):
        fo_copy(j).start()
    loads[6].wait()
    for j in range(1, F):
        arrived(fb.at[j], rfo.at[j], sfo.at[0])
    abuf[0] = merged(fb, F)[0]

    def a_near(g):
        return remote(abuf.at[0], abuf.at[back(g)], sg.at[0], rg.at[back(g) // N], near[g])

    for g in order:
        a_near(g).start()

    for j in range(1, F):
        q_far(j).wait_send()
        fo_copy(j).wait_send()
    all_sent(qbuf.at[1:G], sp.at[0], rp.at[0])
    all_sent(pbuf.at[1:G], so.at[0], ro.at[0])

    def y_copy(j, u, to):
        return remote(
            ysend.at[j, :, pl.ds(u * per_t, per_t)], fin.at[lax.rem(ten + T - to, T)],
            se.at[0], re.at[0], (pool, to),
        )

    def project(j):
        group_arrived(abuf, rg, sg.at[0], j)
        for c in range(N):
            piece = abuf[j * N + lax.rem(c + N - n, N)].astype(jnp.float32)
            for i in range(F):
                att[(i * N + c) * rows : (i * N + c + 1) * rows] = piece[i]
        halves = []
        for s in range(2):
            parts = [att[pl.ds(s * heads + h, Z, stride=rows), :] for h in range(heads)]
            halves.append(jnp.concatenate(parts, axis=1))
        a = jnp.concatenate(halves, axis=0).astype(jnp.bfloat16)
        ysend[j] = dot(a, w[...]).reshape(2, Z, w.shape[1])
        for u in range(t_per_x):
            to = lax.rem(x + j, X) * t_per_x + u

            @pl.when(to != ten)
            def _():
                y_copy(j, u, to).start()

            @pl.when(to == ten)
            def _():
                fin[0] = ysend[j, :, u * per_t : (u + 1) * per_t]

    project(0)
    loop(1, X, lambda i: project(i + lax.div(i, 2) * (1 - 2 * lax.rem(i, 2))))
    all_sent(abuf.at[1:G], sg.at[0], rg.at[0])
    arrived(fin.at[1:T], re.at[0], se.at[0])
    out_ref[...] = jnp.sum(fin[...], axis=0).astype(jnp.bfloat16)
    all_sent(fin.at[1:T], se.at[0], re.at[0])


def body(X, Z, T, kv_pool, queries, new_kv, block_count, tail_gap, block_place, out_weight):
    blocks, _, tokens, hd2 = kv_pool.shape
    hd = hd2 // 2
    rows = 2 * queries.shape[2]
    reqs = block_count.shape[0]
    columns = out_weight.shape[1]
    F, G = Z // N, X * N
    own_rows, half = blocks * rows, N * F * rows
    dma = pltpu.SemaphoreType.DMA
    bf16, f32, i32 = jnp.bfloat16, jnp.float32, jnp.int32
    args = (
        queries.reshape(rows, hd),
        new_kv.reshape(2, hd2),
        block_count.reshape(1, reqs),
        tail_gap.reshape(1, reqs),
        block_place.reshape(1, block_place.shape[0]),
        kv_pool.reshape(blocks, tokens, hd2),
        out_weight,
    )
    return pl.pallas_call(
        functools.partial(kernel, X, Z, T),
        out_shape=jax.ShapeDtypeStruct((2, reqs // T, columns), bf16),
        in_specs=[pl.BlockSpec(memory_space=pl.ANY)] * 7,
        out_specs=pl.BlockSpec(memory_space=pltpu.VMEM),
        scratch_shapes=[pltpu.VMEM(a.shape, a.dtype) for a in args[1:]]
        + [
            pltpu.VMEM((G, F, rows, hd), bf16),
            pltpu.VMEM((X, own_rows, half), bf16),
            pltpu.VMEM((X, half, own_rows), bf16),
            pltpu.VMEM((own_rows, 128), i32),
            pltpu.VMEM((1, own_rows), f32),
            pltpu.VMEM((blocks, 1, 128), f32),
            pltpu.VMEM((blocks, rows, hd), bf16),
            pltpu.VMEM((blocks, rows, hd), f32),
            pltpu.VMEM((chunks, blocks // chunks, 128), f32),
            pltpu.VMEM((G, F + 1, rows, hd), bf16),
            pltpu.VMEM((G + 1, F + 1, rows, hd), bf16),
            pltpu.VMEM((F, F + 1, rows, hd), bf16),
            pltpu.VMEM((G, F, rows, hd), bf16),
            pltpu.VMEM((Z * rows, hd), f32),
            pltpu.VMEM((X, 2, Z, columns), f32),
            pltpu.VMEM((T, 2, reqs // T, columns), f32),
            dma((7,)),
            dma((F,)), dma((F,)),
            dma((1,)), dma((X,)),
            dma((1,)), dma((X,)),
            dma((F,)), dma((F,)),
            dma((1,)), dma((X,)),
            dma((1,)), dma((1,)),
        ],
        compiler_params=pltpu.CompilerParams(
            collective_id=0, has_side_effects=True, vmem_limit_bytes=40 * 1024 * 1024
        ),
    )(*[pltpu.with_memory_space_constraint(a, pltpu.HBM) for a in args])


def solution(mesh):
    pools, tensors = mesh.shape["pool"], mesh.shape["tensor"]
    Z = 16
    placed = (
        P("pool", "tensor", None, None),
        P(None, "pool", "tensor", None),
        P(None, "pool", "tensor", None),
        P(),
        P(),
        P(),
        P("tensor", "pool"),
    )
    return jax.shard_map(
        functools.partial(body, pools // Z, Z, tensors),
        mesh=mesh, in_specs=placed, out_specs=P(None, "tensor", "pool"), check_vma=False,
    )
```

```python
import functools

import jax
import jax.numpy as jnp
from jax import lax
from jax.experimental import pallas as pl
from jax.experimental.pallas import tpu as pltpu
from jax.sharding import PartitionSpec as P

MESH = pl.DeviceIdType.MESH
masked_value = -1e30
N = 4
chunks = 2


def iota(shape, axis):
    return lax.broadcasted_iota(jnp.int32, shape, axis)


def reals(shape, axis):
    return iota(shape, axis).astype(jnp.float32)


def block_tables(bp, cnt, gap, ids, tokens):
    reqs = cnt.shape[1]
    blocks = ids.shape[0]
    rank = jnp.sum(jnp.where(bp == ids, reals((blocks, bp.shape[1]), 1), 0.0), axis=1, keepdims=True)
    row, col = iota((reqs, reqs), 0), iota((reqs, reqs), 1)
    cnt_col = jnp.sum(jnp.where(row == col, cnt, 0.0), axis=1, keepdims=True)
    ends = jnp.sum(jnp.where(row <= col, cnt_col, 0.0), axis=0, keepdims=True)
    request = jnp.sum(jnp.where(ends <= rank, 1.0, 0.0), axis=1, keepdims=True)
    offset = cnt * tokens - 2.0 - gap + (ends - cnt) * tokens
    picked = jnp.sum(
        jnp.where(reals((blocks, reqs), 1) == request, offset, 0.0), axis=1, keepdims=True
    )
    return request, picked - rank * tokens


def to_column(values, count, rows):
    shape = (count, rows, 128)
    return jnp.sum(
        jnp.where(iota(shape, 2) == iota(shape, 1), jnp.broadcast_to(values, shape), 0.0),
        axis=2, keepdims=True,
    )


def in_three(values, rows):
    high = values.astype(jnp.bfloat16).astype(jnp.float32)
    middle = (values - high).astype(jnp.bfloat16).astype(jnp.float32)
    low = values - high - middle
    row = iota((rows, 128), 0)
    tile = jnp.where(row == 0, high, jnp.where(row == 1, middle, jnp.where(row == 2, low, 0.0)))
    return tile.astype(jnp.bfloat16)


def kernel(
    X, Z, T,
    q_hbm, nk_hbm, cnt_hbm, gap_hbm, bp_hbm, kv_hbm, w_hbm, out_ref,
    nk_ref, cnt_ref, gap_ref, bp_ref, kv, w,
    qbuf, pick_ref, put_ref, slot_ref, goes_ref, limit_ref, qsel_ref, out_blocks, lse_ref, pbuf, rbuf, fb, abuf, att, ysend, fin,
    sem_in, sf, rf, sp, rp, so, ro, sfo, rfo, sg, rg, se, re,
):
    pool, ten = lax.axis_index("pool"), lax.axis_index("tensor")
    x, z = lax.div(pool, Z), lax.rem(pool, Z)
    F = Z // N
    G = X * N
    n, f = lax.rem(z, N), lax.div(z, N)
    blocks, tokens, hd2 = kv.shape
    hd = hd2 // 2
    rows = q_hbm.shape[0]
    reqs = cnt_ref.shape[1]
    per_t = reqs // T
    t_per_x = Z // per_t
    heads = rows // 2
    scale = hd ** (-0.5)
    frows = F * rows

    xs = [x] + [lax.rem(x + j, X) for j in range(1, X)]
    hops = [[0, 1, 2, Z - 1], [0, 1, Z - 2, Z - 1]]
    zs = {h: z if h == 0 else lax.rem(z + h, Z) for h in set(hops[0] + hops[1])}
    far = [(x * Z + lax.rem(z + N * j, Z), ten) for j in range(F)]
    near = [(xs[g // N] * Z + zs[hops[g // N % 2][g % N]], ten) for g in range(G)]
    sides = [(pool, lax.rem(ten + j, T)) for j in range(T)]

    def back(g):
        return ((X - g // N) % X) * N + (N - g % N) % N

    order = sorted(range(1, G), key=lambda g: -(min(g // N, X - g // N) + [0, 1, 2, 1][g % N]))

    def remote(src, dst, send, recv, device):
        return pltpu.make_async_remote_copy(
            src_ref=src, dst_ref=dst, send_sem=send, recv_sem=recv,
            device_id=device, device_id_type=MESH,
        )

    def arrived(dst, recv, send):
        remote(dst, dst, send, recv, far[1]).wait_recv()

    pairs = [
        (q_hbm, qbuf.at[0, f]), (bp_hbm, bp_ref), (cnt_hbm, cnt_ref), (gap_hbm, gap_ref),
        (nk_hbm, nk_ref), (kv_hbm, kv), (w_hbm, w),
    ]
    loads = [pltpu.make_async_copy(a, b, sem_in.at[i]) for i, (a, b) in enumerate(pairs)]
    loads[0].start()
    barrier = pltpu.get_barrier_semaphore()
    for device in far[1:] + near[1:] + sides[1:]:
        pl.semaphore_signal(barrier, inc=1, device_id=device, device_id_type=MESH)
    for load in loads[1:]:
        load.start()
    loads[0].wait()
    pl.semaphore_wait(barrier, F + G + T - 3)

    def group(buf, j):
        if isinstance(j, int):
            return buf.at[max(j * N, 1) : (j + 1) * N]
        return buf.at[pl.ds(j * N, N)]

    def loop(low, high, body):
        def once(i, carry):
            body(i)
            return carry

        lax.fori_loop(low, high, once, 0)

    def group_arrived(buf, recv, send, j):
        here = group(buf, j)
        remote(here, here, send, recv.at[j], far[1]).wait_recv()

    def all_sent(part, send, recv):
        remote(part, part, send, recv, far[1]).wait_send()

    def q_far(j):
        return remote(qbuf.at[0, f], qbuf.at[0, f], sf.at[j], rf.at[f], far[j])

    def q_near(g):
        return remote(qbuf.at[0], qbuf.at[back(g)], sp.at[0], rp.at[back(g) // N], near[g])

    for j in range(1, F):
        q_far(j).start()

    for j in range(1, F):
        at = lax.rem(f + j, F)
        arrived(qbuf.at[0, at], rf.at[at], sf.at[0])
    for g in order:
        q_near(g).start()

    for load in loads[1:5]:
        load.wait()
    cnt = cnt_ref[...].astype(jnp.float32)
    gap = gap_ref[...].astype(jnp.float32)
    ids = pool * blocks + iota((blocks, 1), 0)
    request, usable = block_tables(bp_ref[...], cnt, gap, ids, float(tokens))
    asked = request.astype(jnp.int32)
    asked_x = lax.shift_right_logical(asked, Z.bit_length() - 1)
    slot = (
        jnp.bitwise_and(asked_x - x, X - 1) * N + jnp.bitwise_and(asked - z, N - 1)
    ) * F + lax.shift_right_logical(jnp.bitwise_and(asked, Z - 1), N.bit_length() - 1)

    for b in range(blocks):
        limit_ref[b] = jnp.broadcast_to(usable[b : b + 1], (1, 128))

    own_rows = blocks * rows
    all_rows = G * frows
    slot_row = (
        jnp.broadcast_to((slot * rows)[:, None, :], (blocks, rows, 1)) + iota((blocks, rows, 1), 1)
    ).reshape(own_rows, 1)
    half = G * F * rows // X
    slot_ref[...] = jnp.broadcast_to(slot_row, (own_rows, 128))

    def fill_pick(j):
        here = slot_ref[...][:, :1] - j * half == iota((own_rows, half), 1)
        pick_ref[j] = jnp.where(here, 1.0, 0.0).astype(jnp.bfloat16)

    loop(0, X, fill_pick)

    lane = iota((rows, 128), 1)
    spread = jnp.bitwise_and(lane, rows - 1) == iota((rows, 128), 0)
    slot_lane = jnp.sum(
        jnp.where(
            lax.shift_right_logical(iota((blocks, own_rows), 1), rows.bit_length() - 1)
            == iota((blocks, own_rows), 0),
            slot, 0,
        ).astype(jnp.float32),
        axis=0, keepdims=True,
    )
    goes_to = slot_lane * rows + jnp.bitwise_and(iota((1, own_rows), 1), rows - 1).astype(
        jnp.float32
    )
    goes_ref[...] = goes_to

    def fill_put(j):
        here = goes_ref[...] - (j * half).astype(jnp.float32) == reals((half, own_rows), 0)
        put_ref[j] = jnp.where(here, 1.0, 0.0).astype(jnp.bfloat16)

    loop(0, X, fill_put)

    def dot(a, c):
        return jnp.dot(a, c, preferred_element_type=jnp.float32)

    def column(j):
        group_arrived(qbuf, rp, sp.at[0], j)
        return dot(pick_ref[j], qbuf[j * N : (j + 1) * N].reshape(half, hd))

    nearest = sorted(range(X), key=lambda j: min(j, X - j))
    q_sel = column(0)
    for j in nearest[1:]:
        q_sel += column(j)
    qsel_ref[...] = q_sel.astype(jnp.bfloat16).reshape(blocks, rows, hd)

    loads[5].wait()
    step = blocks // chunks
    position = reals((step, rows, tokens), 2)

    def attend(c):
        part = pl.ds(c * step, step)
        scores = jnp.einsum(
            "bqd,btd->bqt", qsel_ref[part], kv[part, :, :hd], preferred_element_type=jnp.float32
        ) * scale
        limit = jnp.broadcast_to(limit_ref[part], (step, 1, 128))
        limit = jnp.concatenate([limit] * (tokens // 128), axis=2)
        scores = jnp.where(position < limit, scores, masked_value)
        top = jnp.max(scores, axis=2, keepdims=True)
        weights = jnp.exp(scores - top)
        total = jnp.sum(weights, axis=2, keepdims=True)
        out = jnp.einsum(
            "bqt,btd->bqd", weights.astype(jnp.bfloat16), kv[part, :, hd:],
            preferred_element_type=jnp.float32,
        )
        out_blocks[part] = out / total
        lse_ref[c] = jnp.sum(jnp.where(spread[None], top + jnp.log(total), 0.0), axis=1)

    loop(0, chunks, attend)
    out = out_blocks[...]
    lse = lse_ref[...].reshape(blocks, 128)

    def o_copy(g):
        return remote(pbuf.at[g], rbuf.at[back(g)], so.at[0], ro.at[back(g) // N], near[g])

    wanted = jnp.broadcast_to(request, (blocks, 128))
    best = lse
    for k in range(blocks):
        best = jnp.maximum(
            best, jnp.where(wanted == wanted[k : k + 1], lse[k : k + 1], masked_value)
        )
    factor = jnp.exp(lse - best)
    total = jnp.zeros((blocks, 128), jnp.float32)
    for k in range(blocks):
        total += jnp.where(wanted == wanted[k : k + 1], factor[k : k + 1], 0.0)
    lse = best + jnp.log(total)
    slots = jnp.broadcast_to(slot, (blocks, 128))
    sub = lax.shift_right_logical(iota((blocks, 128), 1), rows.bit_length() - 1)
    for g in order + [0]:
        row = jnp.max(jnp.where(slots - g * F == sub, lse, masked_value), axis=0, keepdims=True)
        pbuf[g, F] = in_three(row, rows)
    scaled = (out * to_column((factor / total)[:, None, :], blocks, rows)).reshape(own_rows, hd)
    high = scaled.astype(jnp.bfloat16)
    low = (scaled - high.astype(jnp.float32)).astype(jnp.bfloat16)
    both = jnp.concatenate([high, low], axis=1)
    for j in nearest[::-1]:
        put = dot(put_ref[j], both)
        pbuf[j * N : (j + 1) * N, :F] = (
            (put[:, :hd] + put[:, hd:]).astype(jnp.bfloat16).reshape(N, F, rows, hd)
        )
        for g in order:
            if g // N == j:
                o_copy(g).start()
    rbuf[0] = pbuf[0]

    q_own = qbuf[0, f].astype(jnp.float32)
    new = nk_ref[...].astype(jnp.float32)
    score0 = jnp.sum(q_own * new[0:1, :hd], axis=1, keepdims=True) * scale
    score1 = jnp.sum(q_own * new[1:2, :hd], axis=1, keepdims=True) * scale
    score1 = jnp.where(iota((rows, 1), 0) >= heads, score1, masked_value)
    new_max = jnp.maximum(score0, score1)
    weight0, weight1 = jnp.exp(score0 - new_max), jnp.exp(score1 - new_max)
    new_sum = weight0 + weight1
    new_out = (
        weight0.astype(jnp.bfloat16).astype(jnp.float32) * new[0:1, hd:]
        + weight1.astype(jnp.bfloat16).astype(jnp.float32) * new[1:2, hd:]
    ) / new_sum
    new_lse = jnp.sum(
        jnp.where(spread, new_max + jnp.log(new_sum), 0.0), axis=0, keepdims=True
    )
    rbuf[G] = jnp.zeros((F + 1, rows, hd), jnp.bfloat16)
    new_lse = jnp.where(lax.div(iota((1, 128), 1), rows) == f, new_lse, masked_value)
    rbuf[G, F] = in_three(new_lse, rows)
    rbuf[G, f] = new_out.astype(jnp.bfloat16)

    def merged(buf, count):
        values = jnp.sum(buf[:, F].astype(jnp.float32), axis=1, keepdims=True)
        high = jnp.max(values, axis=0, keepdims=True)
        factor = jnp.exp(values - high)
        total = jnp.sum(factor, axis=0, keepdims=True)
        share = to_column(factor / total, count, frows)
        acc = share[0] * buf[0, :F].astype(jnp.float32).reshape(frows, hd)
        for g in range(1, count):
            acc += share[g] * buf[g, :F].astype(jnp.float32).reshape(frows, hd)
        return acc.astype(jnp.bfloat16).reshape(F, rows, hd), high[0] + jnp.log(total[0])

    for j in nearest:
        group_arrived(rbuf, ro, so.at[0], j)
    out, lse = merged(rbuf, G + 1)
    fb[0, :F] = out
    fb[0, F] = in_three(lse, rows)

    def fo_copy(j):
        return remote(fb.at[0], fb.at[F - j], sfo.at[j], rfo.at[F - j], far[j])

    for j in range(1, F):
        fo_copy(j).start()
    loads[6].wait()
    for j in range(1, F):
        arrived(fb.at[j], rfo.at[j], sfo.at[0])
    abuf[0] = merged(fb, F)[0]

    def a_near(g):
        return remote(abuf.at[0], abuf.at[back(g)], sg.at[0], rg.at[back(g) // N], near[g])

    for g in order:
        a_near(g).start()

    for j in range(1, F):
        q_far(j).wait_send()
        fo_copy(j).wait_send()
    all_sent(qbuf.at[1:G], sp.at[0], rp.at[0])
    all_sent(pbuf.at[1:G], so.at[0], ro.at[0])

    def y_copy(j, u, to):
        return remote(
            ysend.at[j, :, pl.ds(u * per_t, per_t)], fin.at[lax.rem(ten + T - to, T)],
            se.at[0], re.at[0], (pool, to),
        )

    def project(j):
        group_arrived(abuf, rg, sg.at[0], j)
        for c in range(N):
            piece = abuf[j * N + lax.rem(c + N - n, N)].astype(jnp.float32)
            for i in range(F):
                att[(i * N + c) * rows : (i * N + c + 1) * rows] = piece[i]
        halves = []
        for s in range(2):
            parts = [att[pl.ds(s * heads + h, Z, stride=rows), :] for h in range(heads)]
            halves.append(jnp.concatenate(parts, axis=1))
        a = jnp.concatenate(halves, axis=0).astype(jnp.bfloat16)
        ysend[j] = dot(a, w[...]).reshape(2, Z, w.shape[1])
        for u in range(t_per_x):
            to = lax.rem(x + j, X) * t_per_x + u

            @pl.when(to != ten)
            def _():
                y_copy(j, u, to).start()

            @pl.when(to == ten)
            def _():
                fin[0] = ysend[j, :, u * per_t : (u + 1) * per_t]

    project(0)
    loop(1, X, lambda i: project(i + lax.div(i, 2) * (1 - 2 * lax.rem(i, 2))))
    all_sent(abuf.at[1:G], sg.at[0], rg.at[0])
    arrived(fin.at[1:T], re.at[0], se.at[0])
    out_ref[...] = jnp.sum(fin[...], axis=0).astype(jnp.bfloat16)
    all_sent(fin.at[1:T], se.at[0], re.at[0])


def body(X, Z, T, kv_pool, queries, new_kv, block_count, tail_gap, block_place, out_weight):
    blocks, _, tokens, hd2 = kv_pool.shape
    hd = hd2 // 2
    rows = 2 * queries.shape[2]
    reqs = block_count.shape[0]
    columns = out_weight.shape[1]
    F, G = Z // N, X * N
    own_rows, half = blocks * rows, N * F * rows
    dma = pltpu.SemaphoreType.DMA
    bf16, f32, i32 = jnp.bfloat16, jnp.float32, jnp.int32
    args = (
        queries.reshape(rows, hd),
        new_kv.reshape(2, hd2),
        block_count.reshape(1, reqs),
        tail_gap.reshape(1, reqs),
        block_place.reshape(1, block_place.shape[0]),
        kv_pool.reshape(blocks, tokens, hd2),
        out_weight,
    )
    return pl.pallas_call(
        functools.partial(kernel, X, Z, T),
        out_shape=jax.ShapeDtypeStruct((2, reqs // T, columns), bf16),
        in_specs=[pl.BlockSpec(memory_space=pl.ANY)] * 7,
        out_specs=pl.BlockSpec(memory_space=pltpu.VMEM),
        scratch_shapes=[pltpu.VMEM(a.shape, a.dtype) for a in args[1:]]
        + [
            pltpu.VMEM((G, F, rows, hd), bf16),
            pltpu.VMEM((X, own_rows, half), bf16),
            pltpu.VMEM((X, half, own_rows), bf16),
            pltpu.VMEM((own_rows, 128), i32),
            pltpu.VMEM((1, own_rows), f32),
            pltpu.VMEM((blocks, 1, 128), f32),
            pltpu.VMEM((blocks, rows, hd), bf16),
            pltpu.VMEM((blocks, rows, hd), f32),
            pltpu.VMEM((chunks, blocks // chunks, 128), f32),
            pltpu.VMEM((G, F + 1, rows, hd), bf16),
            pltpu.VMEM((G + 1, F + 1, rows, hd), bf16),
            pltpu.VMEM((F, F + 1, rows, hd), bf16),
            pltpu.VMEM((G, F, rows, hd), bf16),
            pltpu.VMEM((Z * rows, hd), f32),
            pltpu.VMEM((X, 2, Z, columns), f32),
            pltpu.VMEM((T, 2, reqs // T, columns), f32),
            dma((7,)),
            dma((F,)), dma((F,)),
            dma((1,)), dma((X,)),
            dma((1,)), dma((X,)),
            dma((F,)), dma((F,)),
            dma((1,)), dma((X,)),
            dma((1,)), dma((1,)),
        ],
        compiler_params=pltpu.CompilerParams(
            collective_id=0, has_side_effects=True, vmem_limit_bytes=40 * 1024 * 1024
        ),
    )(*[pltpu.with_memory_space_constraint(a, pltpu.HBM) for a in args])


def solution(mesh):
    pools, tensors = mesh.shape["pool"], mesh.shape["tensor"]
    Z = 16
    placed = (
        P("pool", "tensor", None, None),
        P(None, "pool", "tensor", None),
        P(None, "pool", "tensor", None),
        P(),
        P(),
        P(),
        P("tensor", "pool"),
    )
    return jax.shard_map(
        functools.partial(body, pools // Z, Z, tensors),
        mesh=mesh, in_specs=placed, out_specs=P(None, "tensor", "pool"), check_vma=False,
    )
```

```python
import functools

import jax
import jax.numpy as jnp
from jax import lax
from jax.experimental import pallas as pl
from jax.experimental.pallas import tpu as pltpu
from jax.sharding import PartitionSpec as P

MESH = pl.DeviceIdType.MESH
masked_value = -1e30
N = 4
chunks = 4


def iota(shape, axis):
    return lax.broadcasted_iota(jnp.int32, shape, axis)


def reals(shape, axis):
    return iota(shape, axis).astype(jnp.float32)


def block_tables(bp, cnt, gap, ids, tokens):
    reqs = cnt.shape[1]
    blocks = ids.shape[0]
    rank = jnp.sum(jnp.where(bp == ids, reals((blocks, bp.shape[1]), 1), 0.0), axis=1, keepdims=True)
    row, col = iota((reqs, reqs), 0), iota((reqs, reqs), 1)
    cnt_col = jnp.sum(jnp.where(row == col, cnt, 0.0), axis=1, keepdims=True)
    ends = jnp.sum(jnp.where(row <= col, cnt_col, 0.0), axis=0, keepdims=True)
    request = jnp.sum(jnp.where(ends <= rank, 1.0, 0.0), axis=1, keepdims=True)
    offset = cnt * tokens - 2.0 - gap + (ends - cnt) * tokens
    picked = jnp.sum(
        jnp.where(reals((blocks, reqs), 1) == request, offset, 0.0), axis=1, keepdims=True
    )
    return request, picked - rank * tokens


def to_column(values, count, rows):
    shape = (count, rows, 128)
    return jnp.sum(
        jnp.where(iota(shape, 2) == iota(shape, 1), jnp.broadcast_to(values, shape), 0.0),
        axis=2, keepdims=True,
    )


def in_three(values, rows):
    high = values.astype(jnp.bfloat16).astype(jnp.float32)
    middle = (values - high).astype(jnp.bfloat16).astype(jnp.float32)
    low = values - high - middle
    row = iota((rows, 128), 0)
    tile = jnp.where(row == 0, high, jnp.where(row == 1, middle, jnp.where(row == 2, low, 0.0)))
    return tile.astype(jnp.bfloat16)


def kernel(
    X, Z, T,
    q_hbm, nk_hbm, cnt_hbm, gap_hbm, bp_hbm, kv_hbm, w_hbm, out_ref,
    nk_ref, cnt_ref, gap_ref, bp_ref, kv, w,
    qbuf, pick_ref, put_ref, slot_ref, goes_ref, limit_ref, pbuf, rbuf, fb, abuf, att, ysend, fin,
    sem_in, sf, rf, sp, rp, so, ro, sfo, rfo, sg, rg, se, re,
):
    pool, ten = lax.axis_index("pool"), lax.axis_index("tensor")
    x, z = lax.div(pool, Z), lax.rem(pool, Z)
    F = Z // N
    G = X * N
    n, f = lax.rem(z, N), lax.div(z, N)
    blocks, tokens, hd2 = kv.shape
    hd = hd2 // 2
    rows = q_hbm.shape[0]
    reqs = cnt_ref.shape[1]
    per_t = reqs // T
    t_per_x = Z // per_t
    heads = rows // 2
    scale = hd ** (-0.5)
    frows = F * rows

    xs = [x] + [lax.rem(x + j, X) for j in range(1, X)]
    hops = [[0, 1, 2, Z - 1], [0, 1, Z - 2, Z - 1]]
    zs = {h: z if h == 0 else lax.rem(z + h, Z) for h in set(hops[0] + hops[1])}
    far = [(x * Z + lax.rem(z + N * j, Z), ten) for j in range(F)]
    near = [(xs[g // N] * Z + zs[hops[g // N % 2][g % N]], ten) for g in range(G)]
    sides = [(pool, lax.rem(ten + j, T)) for j in range(T)]

    def back(g):
        return ((X - g // N) % X) * N + (N - g % N) % N

    order = sorted(range(1, G), key=lambda g: -(min(g // N, X - g // N) + [0, 1, 2, 1][g % N]))

    def remote(src, dst, send, recv, device):
        return pltpu.make_async_remote_copy(
            src_ref=src, dst_ref=dst, send_sem=send, recv_sem=recv,
            device_id=device, device_id_type=MESH,
        )

    def arrived(dst, recv, send):
        remote(dst, dst, send, recv, far[1]).wait_recv()

    pairs = [
        (q_hbm, qbuf.at[0, f]), (bp_hbm, bp_ref), (cnt_hbm, cnt_ref), (gap_hbm, gap_ref),
        (nk_hbm, nk_ref), (kv_hbm, kv), (w_hbm, w),
    ]
    loads = [pltpu.make_async_copy(a, b, sem_in.at[i]) for i, (a, b) in enumerate(pairs)]
    loads[0].start()
    barrier = pltpu.get_barrier_semaphore()
    for device in far[1:] + near[1:] + sides[1:]:
        pl.semaphore_signal(barrier, inc=1, device_id=device, device_id_type=MESH)
    for load in loads[1:]:
        load.start()
    loads[0].wait()
    pl.semaphore_wait(barrier, F + G + T - 3)

    def group(buf, j):
        if isinstance(j, int):
            return buf.at[max(j * N, 1) : (j + 1) * N]
        return buf.at[pl.ds(j * N, N)]

    def loop(low, high, body):
        def once(i, carry):
            body(i)
            return carry

        lax.fori_loop(low, high, once, 0)

    def group_arrived(buf, recv, send, j):
        here = group(buf, j)
        remote(here, here, send, recv.at[j], far[1]).wait_recv()

    def all_sent(part, send, recv):
        remote(part, part, send, recv, far[1]).wait_send()

    def q_far(j):
        return remote(qbuf.at[0, f], qbuf.at[0, f], sf.at[j], rf.at[f], far[j])

    def q_near(g):
        return remote(qbuf.at[0], qbuf.at[back(g)], sp.at[0], rp.at[back(g) // N], near[g])

    for j in range(1, F):
        q_far(j).start()

    for j in range(1, F):
        at = lax.rem(f + j, F)
        arrived(qbuf.at[0, at], rf.at[at], sf.at[0])
    for g in order:
        q_near(g).start()

    for load in loads[1:5]:
        load.wait()
    cnt = cnt_ref[...].astype(jnp.float32)
    gap = gap_ref[...].astype(jnp.float32)
    ids = pool * blocks + iota((blocks, 1), 0)
    request, usable = block_tables(bp_ref[...], cnt, gap, ids, float(tokens))
    asked = request.astype(jnp.int32)
    asked_x = lax.shift_right_logical(asked, Z.bit_length() - 1)
    slot = (
        jnp.bitwise_and(asked_x - x, X - 1) * N + jnp.bitwise_and(asked - z, N - 1)
    ) * F + lax.shift_right_logical(jnp.bitwise_and(asked, Z - 1), N.bit_length() - 1)

    for b in range(blocks):
        limit_ref[b] = jnp.broadcast_to(usable[b : b + 1], (1, 128))

    own_rows = blocks * rows
    all_rows = G * frows
    slot_row = (
        jnp.broadcast_to((slot * rows)[:, None, :], (blocks, rows, 1)) + iota((blocks, rows, 1), 1)
    ).reshape(own_rows, 1)
    half = G * F * rows // X
    slot_ref[...] = jnp.broadcast_to(slot_row, (own_rows, 128))

    def fill_pick(j):
        here = slot_ref[...][:, :1] - j * half == iota((own_rows, half), 1)
        pick_ref[j] = jnp.where(here, 1.0, 0.0).astype(jnp.bfloat16)

    loop(0, X, fill_pick)

    lane = iota((rows, 128), 1)
    spread = jnp.bitwise_and(lane, rows - 1) == iota((rows, 128), 0)
    slot_lane = jnp.sum(
        jnp.where(
            lax.shift_right_logical(iota((blocks, own_rows), 1), rows.bit_length() - 1)
            == iota((blocks, own_rows), 0),
            slot, 0,
        ).astype(jnp.float32),
        axis=0, keepdims=True,
    )
    goes_to = slot_lane * rows + jnp.bitwise_and(iota((1, own_rows), 1), rows - 1).astype(
        jnp.float32
    )
    goes_ref[...] = goes_to

    def fill_put(j):
        here = goes_ref[...] - (j * half).astype(jnp.float32) == reals((half, own_rows), 0)
        put_ref[j] = jnp.where(here, 1.0, 0.0).astype(jnp.bfloat16)

    loop(0, X, fill_put)

    def dot(a, c):
        return jnp.dot(a, c, preferred_element_type=jnp.float32)

    def column(j):
        group_arrived(qbuf, rp, sp.at[0], j)
        return dot(pick_ref[j], qbuf[j * N : (j + 1) * N].reshape(half, hd))

    nearest = sorted(range(X), key=lambda j: min(j, X - j))
    q_sel = column(0)
    for j in nearest[1:]:
        q_sel += column(j)
    q_sel = q_sel.astype(jnp.bfloat16).reshape(blocks, rows, hd)

    loads[5].wait()
    step = blocks // chunks
    position = reals((step, rows, tokens), 2)

    def attend(c):
        part = slice(c * step, (c + 1) * step)
        scores = jnp.einsum(
            "bqd,btd->bqt", q_sel[part], kv[part, :, :hd], preferred_element_type=jnp.float32
        ) * scale
        limit = jnp.broadcast_to(limit_ref[part], (step, 1, 128))
        limit = jnp.concatenate([limit] * (tokens // 128), axis=2)
        scores = jnp.where(position < limit, scores, masked_value)
        top = jnp.max(scores, axis=2, keepdims=True)
        weights = jnp.exp(scores - top)
        total = jnp.sum(weights, axis=2, keepdims=True)
        out = jnp.einsum(
            "bqt,btd->bqd", weights.astype(jnp.bfloat16), kv[part, :, hd:],
            preferred_element_type=jnp.float32,
        )
        return out / total, jnp.sum(jnp.where(spread[None], top + jnp.log(total), 0.0), axis=1)

    out, lse = [jnp.concatenate(a, axis=0) for a in zip(*[attend(c) for c in range(chunks)])]

    def o_copy(g):
        return remote(pbuf.at[g], rbuf.at[back(g)], so.at[0], ro.at[back(g) // N], near[g])

    wanted = jnp.broadcast_to(request, (blocks, 128))
    best = lse
    for k in range(blocks):
        best = jnp.maximum(
            best, jnp.where(wanted == wanted[k : k + 1], lse[k : k + 1], masked_value)
        )
    factor = jnp.exp(lse - best)
    total = jnp.zeros((blocks, 128), jnp.float32)
    for k in range(blocks):
        total += jnp.where(wanted == wanted[k : k + 1], factor[k : k + 1], 0.0)
    lse = best + jnp.log(total)
    slots = jnp.broadcast_to(slot, (blocks, 128))
    sub = lax.shift_right_logical(iota((blocks, 128), 1), rows.bit_length() - 1)
    scaled = (out * to_column((factor / total)[:, None, :], blocks, rows)).reshape(own_rows, hd)
    high = scaled.astype(jnp.bfloat16)
    low = (scaled - high.astype(jnp.float32)).astype(jnp.bfloat16)
    both = jnp.concatenate([high, low], axis=1)
    for j in nearest[::-1]:
        for g in range(j * N, (j + 1) * N):
            row = jnp.max(
                jnp.where(slots - g * F == sub, lse, masked_value), axis=0, keepdims=True
            )
            pbuf[g, F] = in_three(row, rows)
        put = dot(put_ref[j], both)
        pbuf[j * N : (j + 1) * N, :F] = (
            (put[:, :hd] + put[:, hd:]).astype(jnp.bfloat16).reshape(N, F, rows, hd)
        )
        for g in order:
            if g // N == j:
                o_copy(g).start()
    rbuf[0] = pbuf[0]

    q_own = qbuf[0, f].astype(jnp.float32)
    new = nk_ref[...].astype(jnp.float32)
    score0 = jnp.sum(q_own * new[0:1, :hd], axis=1, keepdims=True) * scale
    score1 = jnp.sum(q_own * new[1:2, :hd], axis=1, keepdims=True) * scale
    score1 = jnp.where(iota((rows, 1), 0) >= heads, score1, masked_value)
    new_max = jnp.maximum(score0, score1)
    weight0, weight1 = jnp.exp(score0 - new_max), jnp.exp(score1 - new_max)
    new_sum = weight0 + weight1
    new_out = (
        weight0.astype(jnp.bfloat16).astype(jnp.float32) * new[0:1, hd:]
        + weight1.astype(jnp.bfloat16).astype(jnp.float32) * new[1:2, hd:]
    ) / new_sum
    new_lse = jnp.sum(
        jnp.where(spread, new_max + jnp.log(new_sum), 0.0), axis=0, keepdims=True
    )
    rbuf[G] = jnp.zeros((F + 1, rows, hd), jnp.bfloat16)
    new_lse = jnp.where(lax.div(iota((1, 128), 1), rows) == f, new_lse, masked_value)
    rbuf[G, F] = in_three(new_lse, rows)
    rbuf[G, f] = new_out.astype(jnp.bfloat16)

    def joined(state, buf, first, count):
        values = jnp.sum(buf[first : first + count, F].astype(jnp.float32), axis=1, keepdims=True)
        high = jnp.max(values, axis=0)
        if state is not None:
            high = jnp.maximum(high, state[0])
        factor = jnp.exp(values - high[None])
        total = jnp.sum(factor, axis=0)
        share = to_column(factor, count, frows)
        acc = share[0] * buf[first, :F].astype(jnp.float32).reshape(frows, hd)
        for g in range(1, count):
            acc += share[g] * buf[first + g, :F].astype(jnp.float32).reshape(frows, hd)
        if state is not None:
            old = jnp.exp(state[0] - high)
            total += old * state[1]
            acc += to_column(old[None], 1, frows)[0] * state[2]
        return high, total, acc

    def settled(state):
        out = state[2] * to_column(1.0 / state[1][None], 1, frows)[0]
        return out.astype(jnp.bfloat16).reshape(F, rows, hd)

    state = joined(None, rbuf, G, 1)
    for j in nearest:
        group_arrived(rbuf, ro, so.at[0], j)
        state = joined(state, rbuf, j * N, N)
    fb[0, F] = in_three(state[0] + jnp.log(state[1]), rows)
    fb[0, :F] = settled(state)

    def fo_copy(j):
        return remote(fb.at[0], fb.at[F - j], sfo.at[j], rfo.at[F - j], far[j])

    for j in range(1, F):
        fo_copy(j).start()
    loads[6].wait()
    state = joined(None, fb, 0, 1)
    for j in (1, 3, 2):
        arrived(fb.at[j], rfo.at[j], sfo.at[0])
        state = joined(state, fb, j, 1)
    abuf[0] = settled(state)

    def a_near(g):
        return remote(abuf.at[0], abuf.at[back(g)], sg.at[0], rg.at[back(g) // N], near[g])

    for g in order:
        a_near(g).start()

    for j in range(1, F):
        q_far(j).wait_send()
        fo_copy(j).wait_send()
    all_sent(qbuf.at[1:G], sp.at[0], rp.at[0])
    all_sent(pbuf.at[1:G], so.at[0], ro.at[0])

    def y_copy(j, u, to):
        return remote(
            ysend.at[j, :, pl.ds(u * per_t, per_t)], fin.at[lax.rem(ten + T - to, T)],
            se.at[0], re.at[0], (pool, to),
        )

    def project(j):
        group_arrived(abuf, rg, sg.at[0], j)
        for c in range(N):
            piece = abuf[j * N + lax.rem(c + N - n, N)].astype(jnp.float32)
            for i in range(F):
                att[(i * N + c) * rows : (i * N + c + 1) * rows] = piece[i]
        halves = []
        for s in range(2):
            parts = [att[pl.ds(s * heads + h, Z, stride=rows), :] for h in range(heads)]
            halves.append(jnp.concatenate(parts, axis=1))
        a = jnp.concatenate(halves, axis=0).astype(jnp.bfloat16)
        ysend[j] = dot(a, w[...]).reshape(2, Z, w.shape[1])
        for u in range(t_per_x):
            to = lax.rem(x + j, X) * t_per_x + u

            @pl.when(to != ten)
            def _():
                y_copy(j, u, to).start()

            @pl.when(to == ten)
            def _():
                fin[0] = ysend[j, :, u * per_t : (u + 1) * per_t]

    project(0)
    loop(1, X, lambda i: project(i + lax.div(i, 2) * (1 - 2 * lax.rem(i, 2))))
    all_sent(abuf.at[1:G], sg.at[0], rg.at[0])
    arrived(fin.at[1:T], re.at[0], se.at[0])
    out_ref[...] = jnp.sum(fin[...], axis=0).astype(jnp.bfloat16)
    all_sent(fin.at[1:T], se.at[0], re.at[0])


def body(X, Z, T, kv_pool, queries, new_kv, block_count, tail_gap, block_place, out_weight):
    blocks, _, tokens, hd2 = kv_pool.shape
    hd = hd2 // 2
    rows = 2 * queries.shape[2]
    reqs = block_count.shape[0]
    columns = out_weight.shape[1]
    F, G = Z // N, X * N
    own_rows, half = blocks * rows, N * F * rows
    dma = pltpu.SemaphoreType.DMA
    bf16, f32, i32 = jnp.bfloat16, jnp.float32, jnp.int32
    args = (
        queries.reshape(rows, hd),
        new_kv.reshape(2, hd2),
        block_count.reshape(1, reqs),
        tail_gap.reshape(1, reqs),
        block_place.reshape(1, block_place.shape[0]),
        kv_pool.reshape(blocks, tokens, hd2),
        out_weight,
    )
    return pl.pallas_call(
        functools.partial(kernel, X, Z, T),
        out_shape=jax.ShapeDtypeStruct((2, reqs // T, columns), bf16),
        in_specs=[pl.BlockSpec(memory_space=pl.ANY)] * 7,
        out_specs=pl.BlockSpec(memory_space=pltpu.VMEM),
        scratch_shapes=[pltpu.VMEM(a.shape, a.dtype) for a in args[1:]]
        + [
            pltpu.VMEM((G, F, rows, hd), bf16),
            pltpu.VMEM((X, own_rows, half), bf16),
            pltpu.VMEM((X, half, own_rows), bf16),
            pltpu.VMEM((own_rows, 128), i32),
            pltpu.VMEM((1, own_rows), f32),
            pltpu.VMEM((blocks, 1, 128), f32),
            pltpu.VMEM((G, F + 1, rows, hd), bf16),
            pltpu.VMEM((G + 1, F + 1, rows, hd), bf16),
            pltpu.VMEM((F, F + 1, rows, hd), bf16),
            pltpu.VMEM((G, F, rows, hd), bf16),
            pltpu.VMEM((Z * rows, hd), f32),
            pltpu.VMEM((X, 2, Z, columns), f32),
            pltpu.VMEM((T, 2, reqs // T, columns), f32),
            dma((7,)),
            dma((F,)), dma((F,)),
            dma((1,)), dma((X,)),
            dma((1,)), dma((X,)),
            dma((F,)), dma((F,)),
            dma((1,)), dma((X,)),
            dma((1,)), dma((1,)),
        ],
        compiler_params=pltpu.CompilerParams(
            collective_id=0, has_side_effects=True, vmem_limit_bytes=40 * 1024 * 1024
        ),
    )(*[pltpu.with_memory_space_constraint(a, pltpu.HBM) for a in args])


def solution(mesh):
    pools, tensors = mesh.shape["pool"], mesh.shape["tensor"]
    Z = 16
    placed = (
        P("pool", "tensor", None, None),
        P(None, "pool", "tensor", None),
        P(None, "pool", "tensor", None),
        P(),
        P(),
        P(),
        P("tensor", "pool"),
    )
    return jax.shard_map(
        functools.partial(body, pools // Z, Z, tensors),
        mesh=mesh, in_specs=placed, out_specs=P(None, "tensor", "pool"), check_vma=False,
    )
```
